256 devices in a mesh: gx: 32 (over y, z), gy: 8 (over x, core).
Axes of the slice: x: 4, y: 4, z: 8, core: 2. Of those that a mesh axis runs over, the one named last changes fastest.
Arguments:
- velocities: float32 [3, 32, 8, 20480], P(None, 'gx', 'gy'), may hold values from -6 to 6
- bins: int32 [3, 2, 32, 8, 20480], P(None, None, 'gx', 'gy'), may hold values from 0 to 511, as said below
- offsets: int32 [2, 3], replicated, may hold values from 1 to 3
- axes: int32 [2, 64, 128, 128], P(None, 'gx', 'gy'), may hold values from 0 to 63
- live: int32 [32, 8], P('gx', 'gy'), may hold values from 5120 to 20480, as said below
Outputs:
- new_velocities: float32 [3, 32, 8, 20480], P(None, 'gx', 'gy')
The draws below stay inside these ranges and needn't reach their ends.
Inputs may be any that keep to these rules, and one draw needn't show every extreme that they name: bins[0] lies in 0 .. 7, bins[1] in 0 .. 63, bins[2] in 0 .. 511, uniform over the brick, also in dead slots. `live`: bricks at either x wall are full (20480); occupancy falls towards the middle of the channel to about a third.
All inputs are finite; a program needn't handle non-finite values.
Results may differ from the reference program's by a relative error of at most 0.0001.
Values sent between devices are 32-bit elements; how exact they have to be, the bound alone decides.
No kernel may reach another device: no remote copies, remote signals or barrier semaphores. Data moves between devices by JAX's collectives and lax.ppermute only.
A program may use at most 64 MiB of HBM per device.

```python
import math
import jax
import jax.numpy as jnp
from jax import lax

CX = 2
CY = 16
NZ = 128
FINE = 4
NAXES = 64
STEPS = 2
PMAX = 20480
NX = 64
NY = 128
N_GX = 32
N_GY = 8


def draw_bins(key, part):
    key = jax.random.fold_in(key, 11)
    key_x, key_y, key_z = jax.random.split(key, 3)
    shape = (STEPS, N_GX, N_GY, PMAX)
    fine_x = jax.random.randint(key_x, shape, 0, FINE * CX, dtype=jnp.int32)
    fine_y = jax.random.randint(key_y, shape, 0, FINE * CY, dtype=jnp.int32)
    fine_z = jax.random.randint(key_z, shape, 0, FINE * NZ, dtype=jnp.int32)
    return jnp.stack([fine_x, fine_y, fine_z], axis=0)


def draw_live(key, part):
    key = jax.random.fold_in(key, 23)
    row = jnp.arange(N_GX, dtype=jnp.int32)
    distance = jnp.minimum(row, N_GX - 1 - row)
    halfway = max(N_GX // 2 - 1, 1)
    falloff = 2 * PMAX // 3 * distance // halfway
    jitter = jax.random.randint(key, (N_GX, N_GY), 0, PMAX // 32 + 1, dtype=jnp.int32)
    counts = PMAX - falloff[:, None] - jnp.where(distance[:, None] > 0, jitter, 0)
    return counts.astype(jnp.int32)


def with_ends(entries, own_key, least, top_value):
    extent = entries.shape
    place = [jax.random.randint(jax.random.fold_in(own_key, axis), (), 0, extent[axis]) for axis in range(len(extent))]
    entries = entries.at[tuple(place)].set(least)
    longest = extent.index(max(extent))
    place[longest] = (place[longest] + 1) % extent[longest]
    return entries.at[tuple(place)].set(top_value)


def levels(stream_key, dims, pieces, low, largest):
    factor_of, own = 1.0, jax.random.fold_in(stream_key, 6)
    for position, parts in pieces:
        heights = jnp.exp(jax.random.uniform(jax.random.fold_in(own, position), (parts,), jnp.float32, low / len(pieces), largest / len(pieces)))
        factor_of = factor_of * jnp.repeat(heights, dims[position] // parts).reshape([-1 if axis == position else 1 for axis in range(len(dims))])
    return factor_of


def bell_draw(rng, extent, deviation, limit, cuts=(), kind=jnp.bfloat16):
    entries = jax.random.normal(rng, extent, jnp.float32) * deviation
    if len(cuts) > 0:
        entries = levels(rng, extent, cuts, -0.22, 0.18) * entries
    return jnp.clip(entries, min=-limit, max=limit).astype(kind)


def setup_inputs(seed: int = 0) -> dict:
    key_of = jax.random.split(jax.random.key(seed), 6)
    velocities = bell_draw(key_of[0], (3, N_GX, N_GY, PMAX), 1.0, 6.0, ((1, 32), (2, 8)), jnp.float32)
    bins = draw_bins(jax.random.fold_in(key_of[5], 71), 0)
    offsets = with_ends(jax.random.randint(key_of[2], (STEPS, 3), 1, FINE), jax.random.fold_in(key_of[2], 1), 1, FINE - 1).astype(jnp.int32)
    axes = with_ends(jax.random.randint(key_of[3], (STEPS, NX, NY, NZ), 0, NAXES), jax.random.fold_in(key_of[3], 1), 0, NAXES - 1).astype(jnp.int32)
    live = draw_live(jax.random.fold_in(key_of[5], 71), 0)
    return {"velocities": velocities, "bins": bins, "offsets": offsets, "axes": axes, "live": live}


turn_cos = math.cos(130.0 * math.pi / 180.0)
turn_sin = math.sin(130.0 * math.pi / 180.0)
golden = math.pi * (3.0 - math.sqrt(5.0))

def axis_table(count):
    index = jnp.arange(count, dtype=jnp.int32).astype(jnp.float32)
    height = 1.0 - (2.0 * index + 1.0) / count
    radius = jnp.sqrt(1.0 - height * height)
    angle = index * golden
    return jnp.stack([radius * jnp.cos(angle), radius * jnp.sin(angle), height], axis=0)

def rotate(velocity, mean, axis):
    rel = velocity - mean
    cross = jnp.stack([axis[1] * rel[2] - axis[2] * rel[1], axis[2] * rel[0] - axis[0] * rel[2], axis[0] * rel[1] - axis[1] * rel[0]], axis=0)
    along = lax.optimization_barrier(jnp.sum(axis * rel, axis=0))
    return mean + turn_cos * rel + turn_sin * cross + (1.0 - turn_cos) * along[None] * axis

def reference(velocities, bins, offsets, axes, live):
    table = axis_table(NAXES)
    brick_x = jnp.arange(N_GX, dtype=jnp.int32)[:, None, None]
    brick_y = jnp.arange(N_GY, dtype=jnp.int32)[None, :, None]
    slot = jnp.arange(PMAX, dtype=jnp.int32)[None, None, :]
    alive = (slot < live[:, :, None]).reshape(-1)
    weight = alive.astype(jnp.float32)
    ncell = NX * NY * NZ
    vel = velocities.reshape(3, -1)
    for step in range(STEPS):
        fine_x = bins[0, step] + FINE * CX * brick_x
        fine_y = bins[1, step] + FINE * CY * brick_y
        fine_z = bins[2, step]
        cell_x = jnp.minimum((fine_x + offsets[step, 0]) // FINE, NX - 1)
        cell_y = (fine_y + offsets[step, 1]) // FINE % NY
        cell_z = (fine_z + offsets[step, 2]) // FINE % NZ
        cell = ((cell_x * NY + cell_y) * NZ + cell_z).reshape(-1).astype(jnp.int32)
        count = jax.ops.segment_sum(weight, cell, ncell)
        moment = jnp.stack([jax.ops.segment_sum(weight * vel[c], cell, ncell) for c in range(3)], axis=0)
        mean = moment / jnp.maximum(count, 1.0)[None]
        axis_cells = jnp.take(table, axes[step].reshape(-1), axis=1)
        part_mean = jnp.take(mean, cell, axis=1)
        part_axis = jnp.take(axis_cells, cell, axis=1)
        turned = rotate(vel, part_mean, part_axis)
        vel = jnp.where(alive[None], turned, vel)
    return vel.reshape(3, N_GX, N_GY, PMAX)
```

```python
import functools
import math

import jax
import jax.numpy as jnp
import numpy as np
from jax import lax
from jax.experimental import pallas as pl
from jax.experimental.pallas import tpu as pltpu
from jax.sharding import PartitionSpec as P

FINE = 4
NAXES = 64
STEPS = 2
SLOTS = 20480
LANES = 128
ROWS = SLOTS // LANES
DEPTH = 128
CELLS_X = 2
CELLS_Y = 16
PAIRS = 9
QUADS = 3 * PAIRS
FACE = 8 * PAIRS
SUMS = 3 * FACE
WIDE = 224
AXROWS = STEPS * CELLS_Y
BLOCK = 16
VMEM_LIMIT = 48 * 1024 * 1024

turn_cos = math.cos(130.0 * math.pi / 180.0)
turn_sin = math.sin(130.0 * math.pi / 180.0)
golden = math.pi * (3.0 - math.sqrt(5.0))


def axis_table():
    index = np.arange(NAXES).astype(np.float32)
    height = (np.float32(1.0) - (np.float32(2.0) * index + np.float32(1.0)) / np.float32(NAXES)).astype(np.float32)
    radius = np.sqrt(np.float32(1.0) - height * height).astype(np.float32)
    angle = (index * np.float32(golden)).astype(np.float64)
    rows = np.stack([radius * np.cos(angle), radius * np.sin(angle), height]).astype(np.float32)
    padded = np.zeros((3, 1, LANES), np.float32)
    padded[:, 0, :NAXES] = rows
    return np.broadcast_to(padded, (3, 8, LANES)).copy()


def row_ids(shape):
    return lax.broadcasted_iota(jnp.int32, shape, 0)


def fill_keys(step, bins_ref, offsets_ref, info_ref, key_ref, quad_ref):
    live = info_ref[0]
    at_wall = info_ref[1]
    shape = (ROWS, LANES)
    cell_x = (bins_ref[0, step] + offsets_ref[step, 0]) >> 2
    cell_x = jnp.where(at_wall > 0, jnp.minimum(cell_x, CELLS_X - 1), cell_x)
    cell_y = (bins_ref[1, step] + offsets_ref[step, 1]) >> 2
    cell_z = ((bins_ref[2, step] + offsets_ref[step, 2]) >> 2) & (DEPTH - 1)
    slot = jnp.where(cell_x == 1, 2, cell_x >> 1)
    particle = row_ids(shape) * LANES + lax.broadcasted_iota(jnp.int32, shape, 1)
    quad = slot * PAIRS + (cell_y >> 1)
    key_ref[...] = ((cell_y & 1) * DEPTH + cell_z).astype(jnp.float32)
    quad_ref[...] = jnp.where(particle < live, quad, 100).astype(jnp.float32)


def hot_block(key_ref, base, count):
    ids = [(row_ids((16, LANES)) + 16 * t).astype(jnp.float32).astype(jnp.bfloat16) for t in range(16)]
    one = jnp.ones((16, LANES), jnp.bfloat16)
    zero = jnp.zeros((16, LANES), jnp.bfloat16)
    cols = []
    for r in range(count):
        key = jnp.broadcast_to(key_ref[pl.ds(base + r, 1), :], (16, LANES)).astype(jnp.bfloat16)
        cols.append(jnp.concatenate([jnp.where(key == ids[t], one, zero) for t in range(16)], axis=0))
    return jnp.concatenate(cols, axis=1)


def spread_block(vel_ref, quad_ref, base, count):
    sub = row_ids((8, LANES))
    half = row_ids((16, LANES)) >> 3
    ids = [(half + 2 * t).astype(jnp.float32).astype(jnp.bfloat16) for t in range(WIDE // 16)]
    zero = jnp.zeros((16, LANES), jnp.bfloat16)
    cols = []
    for r in range(count):
        row = pl.ds(base + r, 1)
        part = [jnp.broadcast_to(vel_ref[c, row, :], (8, LANES)) for c in range(3)]
        full = jnp.where((sub == 0) | (sub == 3), part[0], jnp.where((sub == 1) | (sub == 4), part[1], part[2]))
        high = full.astype(jnp.bfloat16).astype(jnp.float32)
        data = jnp.where(sub < 3, high, jnp.where(sub < 6, full - high, jnp.where(sub == 6, 1.0, 0.0)))
        data = jnp.concatenate([data, data], axis=0).astype(jnp.bfloat16)
        quad = jnp.broadcast_to(quad_ref[pl.ds(base + r, 1), :], (16, LANES)).astype(jnp.bfloat16)
        cols.append(jnp.concatenate([jnp.where(quad == ids[t], data, zero) for t in range(WIDE // 16)], axis=0))
    return jnp.concatenate(cols, axis=1)


def add_block(acc_ref, spread, hot):
    acc_ref[...] += lax.dot_general(spread, hot, (((1,), (1,)), ((), ())), preferred_element_type=jnp.float32)


def finish_sums(acc_ref, sums_ref):
    sub = row_ids((8, LANES))
    for q in range(QUADS):
        halves = []
        for parity in range(2):
            part = acc_ref[8 * q:8 * q + 8, parity * DEPTH:(parity + 1) * DEPTH]
            moved = pltpu.roll(part, 5, 0)
            halves.append(jnp.where(sub < 3, part + moved, moved))
        sums_ref[8 * q:8 * q + 8, :] = jnp.where(sub < 4, halves[0], pltpu.roll(halves[1], 4, 0))


def write_faces(info_ref, sums_ref, a_ref, b_ref):
    odd = info_ref[2] > 0
    low = sums_ref[0:FACE, :]
    high = sums_ref[FACE:2 * FACE, :]
    a_ref[0:FACE, :] = jnp.where(odd, high, low)
    b_ref[0:FACE, :] = jnp.where(odd, low, high)


def scatter_kernel(offsets_ref, info_ref, vel_ref, bins_ref, axes_ref, sums_ref, a_ref, b_ref, key_ref, quad_ref, acc_ref):
    fill_keys(0, bins_ref, offsets_ref, info_ref, key_ref, quad_ref)
    acc_ref[...] = jnp.zeros_like(acc_ref)

    def body(turn, carry):
        base = pl.multiple_of(turn * BLOCK, BLOCK)
        add_block(acc_ref, spread_block(vel_ref, quad_ref, base, BLOCK), hot_block(key_ref, base, BLOCK))
        return carry

    lax.fori_loop(0, ROWS // BLOCK, body, 0)
    finish_sums(acc_ref, sums_ref)
    write_faces(info_ref, sums_ref, a_ref, b_ref)
    for step in range(STEPS):
        own = axes_ref[step, 0].astype(jnp.float32)
        a_ref[FACE + step * CELLS_Y:FACE + (step + 1) * CELLS_Y, :] = own
        b_ref[FACE + step * CELLS_Y:FACE + (step + 1) * CELLS_Y, :] = own


def fill_fields(step, info_ref, axes_ref, sums_ref, low_x_ref, high_x_ref, low_y_ref, high_y_ref, axes_x_ref, axes_y_ref, field_ref):
    sub = row_ids((8, LANES))
    field_ref[...] = jnp.zeros_like(field_ref)
    is_count = (sub == 3) | (sub == 7)
    for slot in range(3):
        for pair in range(PAIRS):
            q = slot * PAIRS + pair
            total = sums_ref[8 * q:8 * q + 8, :]
            if slot == 0:
                total = total + low_x_ref[8 * pair:8 * pair + 8, :]
            if slot == 1:
                total = total + high_x_ref[8 * pair:8 * pair + 8, :]
            if pair == 0:
                total = total + jnp.where(sub < 4, low_y_ref[8 * slot:8 * slot + 8, :], 0.0)
            if pair == PAIRS - 1:
                total = total + jnp.where(sub < 4, high_y_ref[8 * slot:8 * slot + 8, :], 0.0)
            count = jnp.where(is_count, total, 0.0)
            count = count + pltpu.roll(count, 7, 0)
            count = count + pltpu.roll(count, 6, 0)
            mean = total / jnp.maximum(count, 1.0)
            high = mean.astype(jnp.bfloat16).astype(jnp.float32)
            rest = mean - high
            index = []
            for parity in range(2):
                column = 2 * pair + parity
                if column == CELLS_Y:
                    row = axes_y_ref[slot:slot + 1, :]
                elif column > CELLS_Y:
                    row = jnp.zeros((1, LANES), jnp.float32)
                elif slot == 1:
                    row = axes_x_ref[column:column + 1, :]
                else:
                    row = axes_ref[step, slot // 2, column:column + 1, :].astype(jnp.float32)
                index.append(jnp.broadcast_to(row, (8, LANES)))
            even = jnp.where(sub < 3, high, jnp.where(sub < 6, pltpu.roll(rest, 3, 0), jnp.where(sub == 6, index[0], 0.0)))
            odd = jnp.where(sub < 3, pltpu.roll(high, 4, 0), jnp.where(sub < 6, pltpu.roll(rest, 7, 0), jnp.where(sub == 6, index[1], 0.0)))
            field_ref[8 * q:8 * q + 8, 0:DEPTH] = even
            field_ref[8 * q:8 * q + 8, DEPTH:2 * DEPTH] = odd


def pick_block(picked, quad_ref, got_ref, base, count):
    for r in range(count):
        quad = jnp.broadcast_to(quad_ref[pl.ds(base + r, 1), :], (8, LANES))
        got = jnp.zeros((8, LANES), jnp.float32)
        for q in range(QUADS):
            got = jnp.where(quad == float(q), picked[8 * q:8 * q + 8, r * LANES:(r + 1) * LANES], got)
        got_ref[8 * r:8 * r + 8, :] = got


def turn_block(vel_ref, out_ref, quad_ref, got_ref, table_ref, base, count):
    for g in range(count // 8):
        rows = pl.ds(pl.multiple_of(base + 8 * g, 8), 8)
        chan = [got_ref[pl.ds(64 * g + k, 8, stride=8), :] for k in range(7)]
        mean = [chan[c] + chan[3 + c] for c in range(3)]
        index = chan[6].astype(jnp.int32)
        axis = [jnp.take_along_axis(table_ref[c], index, axis=1, mode="promise_in_bounds") for c in range(3)]
        vel = [vel_ref[c, rows, :] for c in range(3)]
        rel = [vel[c] - mean[c] for c in range(3)]
        along = (1.0 - turn_cos) * (axis[0] * rel[0] + axis[1] * rel[1] + axis[2] * rel[2])
        alive = quad_ref[rows, :] < 64.0
        for c in range(3):
            d, e = (c + 1) % 3, (c + 2) % 3
            cross = axis[d] * rel[e] - axis[e] * rel[d]
            turned = mean[c] + turn_cos * rel[c] + turn_sin * cross + along * axis[c]
            out_ref[c, rows, :] = jnp.where(alive, turned, vel[c])


def gather_block(field, hot):
    return lax.dot_general(field, hot, (((1,), (0,)), ((), ())), preferred_element_type=jnp.float32)


def turn_kernel(step, offsets_ref, info_ref, vel_ref, bins_ref, axes_ref, table_ref, sums_ref, low_x_ref, high_x_ref,
                low_y_ref, high_y_ref, axes_x_ref, axes_y_ref, *rest):
    last = step == STEPS - 1
    if last:
        out_ref, key_ref, quad_ref, field_ref, got_ref = rest
    else:
        out_ref, next_ref, a_ref, b_ref, key_ref, quad_ref, field_ref, got_ref, key2_ref, quad2_ref, acc_ref = rest
        fill_keys(step + 1, bins_ref, offsets_ref, info_ref, key2_ref, quad2_ref)
        acc_ref[...] = jnp.zeros_like(acc_ref)
    fill_keys(step, bins_ref, offsets_ref, info_ref, key_ref, quad_ref)
    fill_fields(step, info_ref, axes_ref, sums_ref, low_x_ref, high_x_ref, low_y_ref, high_y_ref, axes_x_ref, axes_y_ref, field_ref)

    def body(turn, carry):
        base = pl.multiple_of(turn * BLOCK, BLOCK)
        field = field_ref[...].astype(jnp.bfloat16)
        picked = gather_block(field, hot_block(key_ref, base, BLOCK))
        pick_block(picked, quad_ref, got_ref, base, BLOCK)
        turn_block(vel_ref, out_ref, quad_ref, got_ref, table_ref, base, BLOCK)
        if not last:
            add_block(acc_ref, spread_block(out_ref, quad2_ref, base, BLOCK), hot_block(key2_ref, base, BLOCK))
        return carry

    lax.fori_loop(0, ROWS // BLOCK, body, 0)
    if not last:
        finish_sums(acc_ref, next_ref)
        write_faces(info_ref, next_ref, a_ref, b_ref)


SMEM = pl.BlockSpec(memory_space=pltpu.SMEM)
VMEM = pl.BlockSpec(memory_space=pltpu.VMEM)


def f32(*shape):
    return jax.ShapeDtypeStruct(shape, jnp.float32)


def particle_scratch():
    return [pltpu.VMEM((ROWS, LANES), jnp.float32), pltpu.VMEM((ROWS, LANES), jnp.float32)]


def scatter_call(offsets, info, vel, bins, axes):
    face = f32(FACE + AXROWS, LANES)
    return pl.pallas_call(
        scatter_kernel,
        out_shape=(f32(SUMS, LANES), face, face),
        in_specs=[SMEM, SMEM, VMEM, VMEM, VMEM],
        out_specs=(VMEM, VMEM, VMEM),
        scratch_shapes=particle_scratch() + [pltpu.VMEM((WIDE, 2 * DEPTH), jnp.float32)],
        compiler_params=pltpu.CompilerParams(vmem_limit_bytes=VMEM_LIMIT),
        name="scatter",
    )(offsets, info, vel, bins, axes)


def turn_call(step, offsets, info, vel, bins, axes, table, *exchanged):
    last = step == STEPS - 1
    out_shape = [f32(3, ROWS, LANES)]
    scratch = particle_scratch() + [
        pltpu.VMEM((WIDE, 2 * DEPTH), jnp.float32),
        pltpu.VMEM((8 * BLOCK, LANES), jnp.float32),
    ]
    if not last:
        out_shape += [f32(SUMS, LANES), f32(FACE, LANES), f32(FACE, LANES)]
        scratch += particle_scratch() + [pltpu.VMEM((WIDE, 2 * DEPTH), jnp.float32)]
    return pl.pallas_call(
        functools.partial(turn_kernel, step),
        out_shape=tuple(out_shape),
        in_specs=[SMEM, SMEM] + [VMEM] * (4 + len(exchanged)),
        out_specs=tuple([VMEM] * len(out_shape)),
        scratch_shapes=scratch,
        compiler_params=pltpu.CompilerParams(vmem_limit_bytes=VMEM_LIMIT),
        name="turn",
    )(offsets, info, vel, bins, axes, table, *exchanged)


def swaps(count_x, count_y):
    x_odd, x_even, y_odd, y_even = [], [], [], []
    for i in range(count_x):
        for j in range(count_y):
            here = i * count_y + j
            up = i + 1 if i % 2 == 1 else i - 1
            x_odd.append((here, up * count_y + j if 0 <= up < count_x else i * count_y + (j ^ 1)))
            x_even.append((here, (i ^ 1) * count_y + j))
            y_odd.append((here, i * count_y + ((j + 1 if j % 2 == 1 else j - 1) % count_y)))
            y_even.append((here, i * count_y + (j ^ 1)))
    return x_odd, x_even, y_odd, y_even


def per_device(perms, velocities, bins, offsets, axes, live):
    names = ("gx", "gy")
    x_odd, x_even, y_odd, y_even = perms
    i, j = lax.axis_index("gx"), lax.axis_index("gy")
    last_i = lax.axis_size("gx") - 1
    odd_x, odd_y = i % 2 == 1, j % 2 == 1
    vel = velocities.reshape(3, ROWS, LANES)
    bins = bins.reshape(3, STEPS, ROWS, LANES)
    info = jnp.stack([live.reshape(()), (i == last_i).astype(jnp.int32), odd_x.astype(jnp.int32), odd_y.astype(jnp.int32)])
    table = jnp.asarray(axis_table())
    sums, a, b = scatter_call(offsets, info, vel, bins, axes)
    axes_x = axes_y = None
    for step in range(STEPS):
        got_b = lax.ppermute(b, names, x_even)
        got_a = lax.ppermute(a, names, x_odd)
        from_low = jnp.where(odd_x, got_b, got_a)
        from_high = jnp.where(odd_x, got_a, got_b)
        low_x = jnp.where(i > 0, from_low[:FACE], 0.0)
        high_x = jnp.where(i < last_i, from_high[:FACE], 0.0)
        if step == 0:
            axes_x = [from_high[FACE + s * CELLS_Y:FACE + (s + 1) * CELLS_Y] for s in range(STEPS)]
        plane_0 = sums[0:FACE] + low_x
        plane_2 = sums[FACE:2 * FACE] + high_x
        plane_1 = sums[2 * FACE:]
        bottom = [p[0:4] for p in (plane_0, plane_2, plane_1)]
        top = [p[4 * CELLS_Y:4 * CELLS_Y + 4] for p in (plane_0, plane_2, plane_1)]
        if step == 0:
            own = axes.astype(jnp.float32)
            for s in range(STEPS):
                rows = [own[s, 0, 0:1], axes_x[s][0:1], own[s, 1, 0:1], jnp.zeros((1, LANES), jnp.float32)]
                bottom += rows
                top += rows
        bottom, top = jnp.concatenate(bottom), jnp.concatenate(top)
        got_d = lax.ppermute(jnp.where(odd_y, bottom, top), names, y_even)
        got_c = lax.ppermute(jnp.where(odd_y, top, bottom), names, y_odd)
        from_low = jnp.where(odd_y, got_d, got_c)
        from_high = jnp.where(odd_y, got_c, got_d)
        if step == 0:
            axes_y = [from_high[12 + 4 * s:16 + 4 * s] for s in range(STEPS)]
        low_y = jnp.pad(from_low[:12].reshape(3, 4, LANES), ((0, 0), (0, 4), (0, 0))).reshape(24, LANES)
        high_y = jnp.pad(from_high[:12].reshape(3, 4, LANES), ((0, 0), (0, 4), (0, 0))).reshape(24, LANES)
        done = turn_call(step, offsets, info, vel, bins, axes, table, sums, low_x, high_x, low_y, high_y, axes_x[step], axes_y[step])
        if step < STEPS - 1:
            vel, sums, a, b = done
        else:
            vel = done[0]
    return vel.reshape(velocities.shape)


def solution(mesh):
    placed = (
        P(None, "gx", "gy", None),
        P(None, None, "gx", "gy", None),
        P(),
        P(None, "gx", "gy", None),
        P("gx", "gy"),
    )
    perms = swaps(mesh.shape["gx"], mesh.shape["gy"])
    return jax.shard_map(
        functools.partial(per_device, perms), mesh=mesh, in_specs=placed, out_specs=P(None, "gx", "gy", None), check_vma=False
    )
```

```python
import functools
import math

import jax
import jax.numpy as jnp
import numpy as np
from jax import lax
from jax.experimental import pallas as pl
from jax.experimental.pallas import tpu as pltpu
from jax.sharding import PartitionSpec as P

NAXES = 64
STEPS = 2
SLOTS = 20480
LANES = 128
ROWS = SLOTS // LANES
DEPTH = 128
CELLS_X = 2
CELLS_Y = 16
PLANE = 18
COLUMNS = 3 * PLANE
PAIRS = COLUMNS // 2
GROUPS = 7
FACE = 4 * PLANE
SUMS = 32 * GROUPS
WIDE = 8 * 28
AXROWS = STEPS * CELLS_Y
BLOCK = 32
DEAD = 64 * DEPTH
VMEM_LIMIT = 40 * 1024 * 1024

turn_cos = math.cos(130.0 * math.pi / 180.0)
turn_sin = math.sin(130.0 * math.pi / 180.0)
golden = math.pi * (3.0 - math.sqrt(5.0))


def axis_table():
    index = np.arange(NAXES).astype(np.float32)
    height = (np.float32(1.0) - (np.float32(2.0) * index + np.float32(1.0)) / np.float32(NAXES)).astype(np.float32)
    radius = np.sqrt(np.float32(1.0) - height * height).astype(np.float32)
    angle = (index * np.float32(golden)).astype(np.float64)
    rows = np.stack([radius * np.cos(angle), radius * np.sin(angle), height]).astype(np.float32)
    padded = np.zeros((3, 1, LANES), np.float32)
    padded[:, 0, :NAXES] = rows
    return np.broadcast_to(padded, (3, 8, LANES)).copy()


def row_ids(shape):
    return lax.broadcasted_iota(jnp.int32, shape, 0)


def cell_code(bins_ref, step, offsets_ref, live, at_wall):
    shape = (ROWS, LANES)
    cell_x = (bins_ref[0] + offsets_ref[step, 0]) >> 2
    cell_x = jnp.where(at_wall, jnp.minimum(cell_x, CELLS_X - 1), cell_x)
    cell_y = (bins_ref[1] + offsets_ref[step, 1]) >> 2
    cell_z = ((bins_ref[2] + offsets_ref[step, 2]) >> 2) & (DEPTH - 1)
    plane = jnp.where(cell_x == 1, 2, cell_x >> 1)
    particle = row_ids(shape) * LANES + lax.broadcasted_iota(jnp.int32, shape, 1)
    code = (plane * PLANE + cell_y) * DEPTH + cell_z
    return jnp.where(particle < live, code, code + DEAD)


def fill_keys(code, key_ref, pair_ref):
    key_ref[...] = (code & 255).astype(jnp.float32)
    pair_ref[...] = (code >> 8).astype(jnp.float32)


def hot_row(key_ref, row):
    key = jnp.broadcast_to(key_ref[row, :], (16, LANES)).astype(jnp.bfloat16)
    one = jnp.ones((16, LANES), jnp.bfloat16)
    zero = jnp.zeros((16, LANES), jnp.bfloat16)
    ids = [(row_ids((16, LANES)) + 16 * t).astype(jnp.float32).astype(jnp.bfloat16) for t in range(16)]
    return jnp.concatenate([jnp.where(key == ids[t], one, zero) for t in range(16)], axis=0)


def spread_row(vel_ref, pair_ref, row):
    sub = row_ids((8, LANES))
    half = row_ids((16, LANES)) >> 3
    zero = jnp.zeros((16, LANES), jnp.bfloat16)
    part = [jnp.broadcast_to(vel_ref[c, row, :], (8, LANES)) for c in range(3)]
    full = jnp.where((sub == 0) | (sub == 3), part[0], jnp.where((sub == 1) | (sub == 4), part[1], part[2]))
    high = full.astype(jnp.bfloat16).astype(jnp.float32)
    data = jnp.where(sub < 3, high, jnp.where(sub < 6, full - high, jnp.where(sub == 6, 1.0, 0.0)))
    data = jnp.concatenate([data, data], axis=0).astype(jnp.bfloat16)
    pair = jnp.broadcast_to(pair_ref[row, :], (16, LANES)).astype(jnp.bfloat16)
    ids = [(half + 2 * t).astype(jnp.float32).astype(jnp.bfloat16) for t in range(WIDE // 16)]
    return jnp.concatenate([jnp.where(pair == ids[t], data, zero) for t in range(WIDE // 16)], axis=0)


def scatter_rows(acc_ref, vel_ref, key_ref, pair_ref, base, count):
    rows = [pl.ds(base + r, 1) for r in range(count)]
    spread = jnp.concatenate([spread_row(vel_ref, pair_ref, row) for row in rows], axis=1)
    hot = jnp.concatenate([hot_row(key_ref, row) for row in rows], axis=1)
    acc_ref[...] += lax.dot_general(spread, hot, (((1,), (1,)), ((), ())), preferred_element_type=jnp.float32)


def finish_sums(acc_ref, sums_ref):
    sub = row_ids((8, LANES))
    for q in range(SUMS // 8):
        halves = []
        for parity in range(2):
            part = acc_ref[8 * q:8 * q + 8, parity * DEPTH:(parity + 1) * DEPTH]
            moved = pltpu.roll(part, 5, 0)
            halves.append(jnp.where(sub < 3, part + moved, moved))
        sums_ref[8 * q:8 * q + 8, :] = jnp.where(sub < 4, halves[0], pltpu.roll(halves[1], 4, 0))


def write_faces(sums_ref, a_ref, b_ref):
    odd = lax.axis_index("gx") % 2 == 1
    low = sums_ref[0:FACE, :]
    high = sums_ref[FACE:2 * FACE, :]
    a_ref[0:FACE, :] = jnp.where(odd, high, low)
    b_ref[0:FACE, :] = jnp.where(odd, low, high)


def scatter_kernel(offsets_hbm, live_hbm, vel_hbm, bins_hbm, axes_hbm, table_hbm,
                   vel_ref, code_ref, axes_ref, table_ref, sums_ref, a_ref, b_ref,
                   bins_ref, key_ref, pair_ref, acc_ref, offsets_ref, live_ref, sems):
    copies = [
        pltpu.make_async_copy(offsets_hbm, offsets_ref, sems.at[0]),
        pltpu.make_async_copy(live_hbm, live_ref, sems.at[1]),
        pltpu.make_async_copy(bins_hbm.at[:, 0], bins_ref.at[0], sems.at[2]),
        pltpu.make_async_copy(vel_hbm, vel_ref, sems.at[3]),
        pltpu.make_async_copy(bins_hbm.at[:, 1], bins_ref.at[1], sems.at[4]),
        pltpu.make_async_copy(axes_hbm, axes_ref, sems.at[5]),
        pltpu.make_async_copy(table_hbm, table_ref, sems.at[6]),
    ]
    for copy in copies:
        copy.start()
    acc_ref[...] = jnp.zeros_like(acc_ref)
    at_wall = lax.axis_index("gx") == lax.axis_size("gx") - 1
    for copy in copies[:3]:
        copy.wait()
    live = live_ref[0, 0]
    code = cell_code(bins_ref.at[0], 0, offsets_ref, live, at_wall)
    code_ref[0] = code
    fill_keys(code, key_ref, pair_ref)
    copies[3].wait()

    def body(turn, carry):
        scatter_rows(acc_ref, vel_ref, key_ref, pair_ref, pl.multiple_of(turn * BLOCK, BLOCK), BLOCK)
        return carry

    lax.fori_loop(0, ROWS // BLOCK, body, 0)
    finish_sums(acc_ref, sums_ref)
    write_faces(sums_ref, a_ref, b_ref)
    for copy in copies[4:]:
        copy.wait()
    code_ref[1] = cell_code(bins_ref.at[1], 1, offsets_ref, live, at_wall)
    for step in range(STEPS):
        own = axes_ref[step, 0].astype(jnp.float32)
        a_ref[FACE + step * CELLS_Y:FACE + (step + 1) * CELLS_Y, :] = own
        b_ref[FACE + step * CELLS_Y:FACE + (step + 1) * CELLS_Y, :] = own


def fill_fields(step, axes_ref, sums_ref, a_ref, b_ref, c_ref, d_ref, first, total_ref, index_ref, packed_ref, mean_ref):
    i, j = lax.axis_index("gx"), lax.axis_index("gy")
    odd_x, odd_y = i % 2 == 1, j % 2 == 1
    first_a, first_b, first_c, first_d = first
    low_x = jnp.where(odd_x, b_ref[0:FACE, :], a_ref[0:FACE, :])
    high_x = jnp.where(odd_x, a_ref[0:FACE, :], b_ref[0:FACE, :])
    total_ref[0:FACE, :] = sums_ref[0:FACE, :] + jnp.where(i > 0, low_x, 0.0)
    total_ref[FACE:2 * FACE, :] = sums_ref[FACE:2 * FACE, :] + jnp.where(i < lax.axis_size("gx") - 1, high_x, 0.0)
    total_ref[2 * FACE:, :] = sums_ref[2 * FACE:, :]
    low_y = jnp.where(odd_y, d_ref[...], c_ref[...])
    high_y = jnp.where(odd_y, c_ref[...], d_ref[...])
    index_ref[...] = jnp.zeros_like(index_ref)
    rows = slice(FACE + step * CELLS_Y, FACE + (step + 1) * CELLS_Y)
    index_ref[0:CELLS_Y, :] = axes_ref[step, 0]
    index_ref[PLANE:PLANE + CELLS_Y, :] = jnp.where(odd_x, first_a[rows, :], first_b[rows, :]).astype(jnp.int32)
    index_ref[2 * PLANE:2 * PLANE + CELLS_Y, :] = axes_ref[step, 1]
    rows = slice(12 + 4 * step, 15 + 4 * step)
    index_y = jnp.where(odd_y, first_c[rows, :], first_d[rows, :]).astype(jnp.int32)
    for plane in range(3):
        top = 4 * (plane * PLANE + CELLS_Y)
        total_ref[plane * FACE:plane * FACE + 4, :] += low_y[4 * plane:4 * plane + 4, :]
        total_ref[top:top + 4, :] += high_y[4 * plane:4 * plane + 4, :]
        index_ref[plane * PLANE + CELLS_Y:plane * PLANE + CELLS_Y + 1, :] = index_y[plane:plane + 1, :]
    first_mean = []
    for g in range(GROUPS):
        count = jnp.maximum(total_ref[pl.ds(32 * g + 3, 8, stride=4), :], 1.0)
        mean = [total_ref[pl.ds(32 * g + c, 8, stride=4), :] / count for c in range(3)]
        first_mean.append(mean[0])
        mean_ref[0, 8 * g:8 * g + 8, :] = mean[1]
        mean_ref[1, 8 * g:8 * g + 8, :] = mean[2]
    largest = functools.reduce(jnp.maximum, [jnp.abs(m) for m in first_mean])
    largest = jnp.maximum(jnp.max(largest, axis=(0, 1), keepdims=True), 1e-30)
    scale = jnp.broadcast_to(2.0 ** 24 / largest, (8, LANES))
    for g in range(GROUPS):
        whole = (first_mean[g] * scale).astype(jnp.int32)
        packed_ref[8 * g:8 * g + 8, :] = whole * NAXES + index_ref[8 * g:8 * g + 8, :]
    return jnp.broadcast_to(largest * 2.0 ** -24, (8, LANES))


def pick(table, index):
    return jnp.take_along_axis(table, index, axis=1, mode="promise_in_bounds")


def turn_rows(vel_ref, out_ref, code_ref, packed_ref, mean_ref, table_ref, unit, got_packed, got_mean, base, count):
    for r in range(count):
        code = jnp.broadcast_to(code_ref[pl.ds(base + r, 1), :], (8, LANES))
        z = code & (DEPTH - 1)
        group = code >> 10
        for g in range(GROUPS):
            rows = slice(8 * g, 8 * g + 8)
            found = [pick(packed_ref[rows, :], z), pick(mean_ref[0, rows, :], z), pick(mean_ref[1, rows, :], z)]
            if g == 0:
                got = found
            else:
                here = group == g
                got = [jnp.where(here, new, old) for new, old in zip(found, got)]
        got_packed[8 * r:8 * r + 8, :] = got[0]
        got_mean[0, 8 * r:8 * r + 8, :] = got[1]
        got_mean[1, 8 * r:8 * r + 8, :] = got[2]
    for b in range(count // 8):
        rows = pl.ds(pl.multiple_of(base + 8 * b, 8), 8)
        code = code_ref[rows, :]
        sub = (code >> 7) & 7
        masks = [sub == k for k in range(8)]

        def choose(ref):
            value = ref[pl.ds(64 * b, 8, stride=8), :]
            for k in range(1, 8):
                value = jnp.where(masks[k], ref[pl.ds(64 * b + k, 8, stride=8), :], value)
            return value

        packed = choose(got_packed)
        index = packed & (NAXES - 1)
        mean = [(packed >> 6).astype(jnp.float32) * unit, choose(got_mean.at[0]), choose(got_mean.at[1])]
        axis = [pick(table_ref[c], index) for c in range(3)]
        vel = [vel_ref[c, rows, :] for c in range(3)]
        rel = [vel[c] - mean[c] for c in range(3)]
        along = (1.0 - turn_cos) * (axis[0] * rel[0] + axis[1] * rel[1] + axis[2] * rel[2])
        for c in range(3):
            d, e = (c + 1) % 3, (c + 2) % 3
            cross = axis[d] * rel[e] - axis[e] * rel[d]
            turned = mean[c] + turn_cos * rel[c] + turn_sin * cross + along * axis[c]
            out_ref[c, rows, :] = jnp.where(code < DEAD, turned, vel[c])


def turn_kernel(step, vel_ref, code_ref, axes_ref, table_ref, sums_ref, a_ref, b_ref, c_ref, d_ref, *rest):
    last = step == STEPS - 1
    if last:
        first = rest[:4]
        out_ref, total_ref, index_ref, packed_ref, mean_ref, got_packed, got_mean = rest[4:]
    else:
        first = (a_ref, b_ref, c_ref, d_ref)
        out_ref, next_ref, na_ref, nb_ref, total_ref, index_ref, packed_ref, mean_ref, got_packed, got_mean, key_ref, pair_ref, acc_ref = rest
        fill_keys(code_ref[step + 1], key_ref, pair_ref)
        acc_ref[...] = jnp.zeros_like(acc_ref)
    unit = fill_fields(step, axes_ref, sums_ref, a_ref, b_ref, c_ref, d_ref, first, total_ref, index_ref, packed_ref, mean_ref)

    def body(turn, carry):
        base = pl.multiple_of(turn * BLOCK, BLOCK)
        turn_rows(vel_ref, out_ref, code_ref.at[step], packed_ref, mean_ref, table_ref, unit, got_packed, got_mean, base, BLOCK)
        if not last:
            scatter_rows(acc_ref, out_ref, key_ref, pair_ref, base, BLOCK)
        return carry

    lax.fori_loop(0, ROWS // BLOCK, body, 0)
    if not last:
        finish_sums(acc_ref, next_ref)
        write_faces(next_ref, na_ref, nb_ref)


HBM = pl.BlockSpec(memory_space=pltpu.HBM)
VMEM = pl.BlockSpec(memory_space=pltpu.VMEM)


def f32(*shape):
    return jax.ShapeDtypeStruct(shape, jnp.float32)


def i32(*shape):
    return jax.ShapeDtypeStruct(shape, jnp.int32)


def scatter_scratch():
    return [
        pltpu.VMEM((ROWS, LANES), jnp.float32),
        pltpu.VMEM((ROWS, LANES), jnp.float32),
        pltpu.VMEM((WIDE, 2 * DEPTH), jnp.float32),
    ]


def scatter_call(offsets, live, vel, bins, axes, table):
    face = f32(FACE + AXROWS, LANES)
    out_shape = (f32(3, ROWS, LANES), i32(STEPS, ROWS, LANES), i32(*axes.shape), f32(3, 8, LANES), f32(SUMS, LANES), face, face)
    return pl.pallas_call(
        scatter_kernel,
        out_shape=out_shape,
        in_specs=[HBM] * 6,
        out_specs=tuple([VMEM] * len(out_shape)),
        scratch_shapes=[pltpu.VMEM((STEPS, 3, ROWS, LANES), jnp.int32)] + scatter_scratch() + [
            pltpu.SMEM((STEPS, 3), jnp.int32),
            pltpu.SMEM((1, 1), jnp.int32),
            pltpu.SemaphoreType.DMA((7,)),
        ],
        compiler_params=pltpu.CompilerParams(vmem_limit_bytes=VMEM_LIMIT),
        name="scatter",
    )(offsets, live, vel, bins, axes, table)


def turn_call(step, *args):
    last = step == STEPS - 1
    out_shape = [f32(3, ROWS, LANES)]
    scratch = [
        pltpu.VMEM((SUMS, LANES), jnp.float32),
        pltpu.VMEM((8 * GROUPS, LANES), jnp.int32),
        pltpu.VMEM((8 * GROUPS, LANES), jnp.int32),
        pltpu.VMEM((2, 8 * GROUPS, LANES), jnp.float32),
        pltpu.VMEM((8 * BLOCK, LANES), jnp.int32),
        pltpu.VMEM((2, 8 * BLOCK, LANES), jnp.float32),
    ]
    if not last:
        out_shape += [f32(SUMS, LANES), f32(FACE, LANES), f32(FACE, LANES)]
        scratch += scatter_scratch()
    return pl.pallas_call(
        functools.partial(turn_kernel, step),
        out_shape=tuple(out_shape),
        in_specs=[VMEM] * len(args),
        out_specs=tuple([VMEM] * len(out_shape)),
        scratch_shapes=scratch,
        compiler_params=pltpu.CompilerParams(vmem_limit_bytes=VMEM_LIMIT),
        name="turn",
    )(*args)


def swaps(count_x, count_y):
    x_odd, x_even, y_odd, y_even = [], [], [], []
    for i in range(count_x):
        for j in range(count_y):
            here = i * count_y + j
            up = i + 1 if i % 2 == 1 else i - 1
            x_odd.append((here, up * count_y + j if 0 <= up < count_x else i * count_y + (j ^ 1)))
            x_even.append((here, (i ^ 1) * count_y + j))
            y_odd.append((here, i * count_y + ((j + 1 if j % 2 == 1 else j - 1) % count_y)))
            y_even.append((here, i * count_y + (j ^ 1)))
    return x_odd, x_even, y_odd, y_even


def y_messages(step, axes, sums, got_a, got_b):
    i = lax.axis_index("gx")
    odd_x = i % 2 == 1
    low_x = jnp.where(odd_x, got_b, got_a)
    high_x = jnp.where(odd_x, got_a, got_b)
    has_low, has_high = i > 0, i < lax.axis_size("gx") - 1
    ends = []
    for start in (0, 4 * CELLS_Y):
        rows = slice(start, start + 4)
        ends.append([
            sums[0:FACE][rows] + jnp.where(has_low, low_x[:FACE][rows], 0.0),
            sums[FACE:2 * FACE][rows] + jnp.where(has_high, high_x[:FACE][rows], 0.0),
            sums[2 * FACE:3 * FACE][rows],
        ])
    if step == 0:
        for s in range(STEPS):
            own = axes[s, :, 0].astype(jnp.float32)
            rows = [own[0:1], high_x[FACE + s * CELLS_Y:FACE + s * CELLS_Y + 1], own[1:2], own[1:2]]
            ends = [end + rows for end in ends]
    return [jnp.concatenate(end) for end in ends]


def per_device(perms, velocities, bins, offsets, axes, live):
    names = ("gx", "gy")
    x_odd, x_even, y_odd, y_even = perms
    odd_y = lax.axis_index("gy") % 2 == 1
    vel, code, axes, table, sums, a, b = scatter_call(
        offsets, live, velocities.reshape(3, ROWS, LANES), bins.reshape(3, STEPS, ROWS, LANES), axes, jnp.asarray(axis_table()))
    first = ()
    for step in range(STEPS):
        got_b = lax.ppermute(b, names, x_even)
        got_a = lax.ppermute(a, names, x_odd)
        bottom, top = y_messages(step, axes, sums, got_a, got_b)
        got_d = lax.ppermute(jnp.where(odd_y, bottom, top), names, y_even)
        got_c = lax.ppermute(jnp.where(odd_y, top, bottom), names, y_odd)
        got = (got_a, got_b, got_c, got_d)
        done = turn_call(step, vel, code, axes, table, sums, *got, *first)
        if step < STEPS - 1:
            vel, sums, a, b = done
            first = got
        else:
            vel = done[0]
    return vel.reshape(velocities.shape)


def solution(mesh):
    placed = (
        P(None, "gx", "gy", None),
        P(None, None, "gx", "gy", None),
        P(),
        P(None, "gx", "gy", None),
        P("gx", "gy"),
    )
    perms = swaps(mesh.shape["gx"], mesh.shape["gy"])
    return jax.shard_map(
        functools.partial(per_device, perms), mesh=mesh, in_specs=placed, out_specs=P(None, "gx", "gy", None), check_vma=False
    )
```

```python
import functools
import math

import jax
import jax.numpy as jnp
import numpy as np
from jax import lax
from jax.experimental import pallas as pl
from jax.experimental.pallas import tpu as pltpu
from jax.sharding import PartitionSpec as P

NAXES = 64
STEPS = 2
SLOTS = 20480
LANES = 128
ROWS = SLOTS // LANES
DEPTH = 128
CELLS_X = 2
CELLS_Y = 16
PLANE = 18
COLUMNS = 3 * PLANE
PAIRS = COLUMNS // 2
GROUPS = 7
FACE = 4 * PLANE
SUMS = 32 * GROUPS
WIDE = 8 * 28
AXROWS = STEPS * CELLS_Y
BLOCK_1 = 160
BLOCK = 80
DEAD = 64 * DEPTH
VMEM_LIMIT = 40 * 1024 * 1024

turn_cos = math.cos(130.0 * math.pi / 180.0)
turn_sin = math.sin(130.0 * math.pi / 180.0)
golden = math.pi * (3.0 - math.sqrt(5.0))


def axis_table():
    index = np.arange(NAXES).astype(np.float32)
    height = (np.float32(1.0) - (np.float32(2.0) * index + np.float32(1.0)) / np.float32(NAXES)).astype(np.float32)
    radius = np.sqrt(np.float32(1.0) - height * height).astype(np.float32)
    angle = (index * np.float32(golden)).astype(np.float64)
    rows = np.stack([radius * np.cos(angle), radius * np.sin(angle), height]).astype(np.float32)
    padded = np.zeros((3, 1, LANES), np.float32)
    padded[:, 0, :NAXES] = rows
    return np.broadcast_to(padded, (3, 8, LANES)).copy()


def row_ids(shape):
    return lax.broadcasted_iota(jnp.int32, shape, 0)


def cell_code(bins_ref, step, offsets_ref, live, at_wall):
    shape = (ROWS, LANES)
    cell_x = (bins_ref[0] + offsets_ref[step, 0]) >> 2
    cell_x = jnp.where(at_wall, jnp.minimum(cell_x, CELLS_X - 1), cell_x)
    cell_y = (bins_ref[1] + offsets_ref[step, 1]) >> 2
    cell_z = ((bins_ref[2] + offsets_ref[step, 2]) >> 2) & (DEPTH - 1)
    plane = jnp.where(cell_x == 1, 2, cell_x >> 1)
    particle = row_ids(shape) * LANES + lax.broadcasted_iota(jnp.int32, shape, 1)
    code = (plane * PLANE + cell_y) * DEPTH + cell_z
    return jnp.where(particle < live, code, code + DEAD)


def fill_keys(code, key_ref, pair_ref):
    key_ref[...] = (code & 255).astype(jnp.float32)
    pair_ref[...] = (code >> 8).astype(jnp.float32)


def hot_row(key_ref, row):
    key = jnp.broadcast_to(key_ref[row, :], (16, LANES)).astype(jnp.bfloat16)
    one = jnp.ones((16, LANES), jnp.bfloat16)
    zero = jnp.zeros((16, LANES), jnp.bfloat16)
    ids = [(row_ids((16, LANES)) + 16 * t).astype(jnp.float32).astype(jnp.bfloat16) for t in range(16)]
    return jnp.concatenate([jnp.where(key == ids[t], one, zero) for t in range(16)], axis=0)


def spread_row(vel_ref, pair_ref, row):
    sub = row_ids((8, LANES))
    half = row_ids((16, LANES)) >> 3
    zero = jnp.zeros((16, LANES), jnp.bfloat16)
    part = [jnp.broadcast_to(vel_ref[c, row, :], (8, LANES)) for c in range(3)]
    full = jnp.where((sub == 0) | (sub == 3), part[0], jnp.where((sub == 1) | (sub == 4), part[1], part[2]))
    high = full.astype(jnp.bfloat16).astype(jnp.float32)
    data = jnp.where(sub < 3, high, jnp.where(sub < 6, full - high, jnp.where(sub == 6, 1.0, 0.0)))
    data = jnp.concatenate([data, data], axis=0).astype(jnp.bfloat16)
    pair = jnp.broadcast_to(pair_ref[row, :], (16, LANES)).astype(jnp.bfloat16)
    ids = [(half + 2 * t).astype(jnp.float32).astype(jnp.bfloat16) for t in range(WIDE // 16)]
    return jnp.concatenate([jnp.where(pair == ids[t], data, zero) for t in range(WIDE // 16)], axis=0)


def scatter_rows(acc_ref, vel_ref, key_ref, pair_ref, base, count):
    rows = [pl.ds(base + r, 1) for r in range(count)]
    spread = jnp.concatenate([spread_row(vel_ref, pair_ref, row) for row in rows], axis=1)
    hot = jnp.concatenate([hot_row(key_ref, row) for row in rows], axis=1)
    acc_ref[...] += lax.dot_general(spread, hot, (((1,), (1,)), ((), ())), preferred_element_type=jnp.float32)


def finish_sums(acc_ref, sums_ref):
    sub = row_ids((8, LANES))
    for q in range(SUMS // 8):
        halves = []
        for parity in range(2):
            part = acc_ref[8 * q:8 * q + 8, parity * DEPTH:(parity + 1) * DEPTH]
            moved = pltpu.roll(part, 5, 0)
            halves.append(jnp.where(sub < 3, part + moved, moved))
        sums_ref[8 * q:8 * q + 8, :] = jnp.where(sub < 4, halves[0], pltpu.roll(halves[1], 4, 0))


def write_faces(sums_ref, a_ref, b_ref):
    odd = lax.axis_index("gx") % 2 == 1
    low = sums_ref[0:FACE, :]
    high = sums_ref[FACE:2 * FACE, :]
    a_ref[0:FACE, :] = jnp.where(odd, high, low)
    b_ref[0:FACE, :] = jnp.where(odd, low, high)


def scatter_kernel(live_ref, offsets_hbm, vel_hbm, bins_hbm, axes_hbm, table_hbm,
                   vel_ref, code_ref, axes_ref, table_ref, sums_ref, a_ref, b_ref,
                   bins_ref, key_ref, pair_ref, acc_ref, offsets_ref, sems):
    copies = [
        pltpu.make_async_copy(offsets_hbm, offsets_ref, sems.at[0]),
        pltpu.make_async_copy(bins_hbm.at[:, 0], bins_ref.at[0], sems.at[1]),
        pltpu.make_async_copy(vel_hbm, vel_ref, sems.at[2]),
        pltpu.make_async_copy(bins_hbm.at[:, 1], bins_ref.at[1], sems.at[3]),
        pltpu.make_async_copy(axes_hbm, axes_ref, sems.at[4]),
        pltpu.make_async_copy(table_hbm, table_ref, sems.at[5]),
    ]
    for copy in copies:
        copy.start()
    acc_ref[...] = jnp.zeros_like(acc_ref)
    at_wall = lax.axis_index("gx") == lax.axis_size("gx") - 1
    for copy in copies[:2]:
        copy.wait()
    live = live_ref[0, 0]
    code = cell_code(bins_ref.at[0], 0, offsets_ref, live, at_wall)
    code_ref[0] = code
    fill_keys(code, key_ref, pair_ref)
    copies[2].wait()

    def body(turn, carry):
        scatter_rows(acc_ref, vel_ref, key_ref, pair_ref, pl.multiple_of(turn * BLOCK_1, BLOCK_1), BLOCK_1)
        return carry

    lax.fori_loop(0, ROWS // BLOCK_1, body, 0)
    finish_sums(acc_ref, sums_ref)
    write_faces(sums_ref, a_ref, b_ref)
    for copy in copies[3:]:
        copy.wait()
    code_ref[1] = cell_code(bins_ref.at[1], 1, offsets_ref, live, at_wall)
    for step in range(STEPS):
        own = axes_ref[step, 0].astype(jnp.float32)
        a_ref[FACE + step * CELLS_Y:FACE + (step + 1) * CELLS_Y, :] = own
        b_ref[FACE + step * CELLS_Y:FACE + (step + 1) * CELLS_Y, :] = own


def fill_fields(step, axes_ref, sums_ref, a_ref, b_ref, c_ref, d_ref, first, total_ref, index_ref, packed_ref, mean_ref):
    i, j = lax.axis_index("gx"), lax.axis_index("gy")
    odd_x, odd_y = i % 2 == 1, j % 2 == 1
    first_a, first_b, first_c, first_d = first
    low_x = jnp.where(odd_x, b_ref[0:FACE, :], a_ref[0:FACE, :])
    high_x = jnp.where(odd_x, a_ref[0:FACE, :], b_ref[0:FACE, :])
    total_ref[0:FACE, :] = sums_ref[0:FACE, :] + jnp.where(i > 0, low_x, 0.0)
    total_ref[FACE:2 * FACE, :] = sums_ref[FACE:2 * FACE, :] + jnp.where(i < lax.axis_size("gx") - 1, high_x, 0.0)
    total_ref[2 * FACE:, :] = sums_ref[2 * FACE:, :]
    low_y = jnp.where(odd_y, d_ref[...], c_ref[...])
    high_y = jnp.where(odd_y, c_ref[...], d_ref[...])
    index_ref[...] = jnp.zeros_like(index_ref)
    rows = slice(FACE + step * CELLS_Y, FACE + (step + 1) * CELLS_Y)
    index_ref[0:CELLS_Y, :] = axes_ref[step, 0]
    index_ref[PLANE:PLANE + CELLS_Y, :] = jnp.where(odd_x, first_a[rows, :], first_b[rows, :]).astype(jnp.int32)
    index_ref[2 * PLANE:2 * PLANE + CELLS_Y, :] = axes_ref[step, 1]
    rows = slice(12 + 4 * step, 15 + 4 * step)
    index_y = jnp.where(odd_y, first_c[rows, :], first_d[rows, :]).astype(jnp.int32)
    for plane in range(3):
        top = 4 * (plane * PLANE + CELLS_Y)
        total_ref[plane * FACE:plane * FACE + 4, :] += low_y[4 * plane:4 * plane + 4, :]
        total_ref[top:top + 4, :] += high_y[4 * plane:4 * plane + 4, :]
        index_ref[plane * PLANE + CELLS_Y:plane * PLANE + CELLS_Y + 1, :] = index_y[plane:plane + 1, :]
    first_mean = []
    for g in range(GROUPS):
        count = jnp.maximum(total_ref[pl.ds(32 * g + 3, 8, stride=4), :], 1.0)
        mean = [total_ref[pl.ds(32 * g + c, 8, stride=4), :] / count for c in range(3)]
        first_mean.append(mean[0])
        mean_ref[0, 8 * g:8 * g + 8, :] = mean[1]
        mean_ref[1, 8 * g:8 * g + 8, :] = mean[2]
    largest = functools.reduce(jnp.maximum, [jnp.abs(m) for m in first_mean])
    largest = jnp.maximum(jnp.max(largest, axis=(0, 1), keepdims=True), 1e-30)
    scale = jnp.broadcast_to(2.0 ** 24 / largest, (8, LANES))
    for g in range(GROUPS):
        whole = (first_mean[g] * scale).astype(jnp.int32)
        packed_ref[8 * g:8 * g + 8, :] = whole * NAXES + index_ref[8 * g:8 * g + 8, :]
    return jnp.broadcast_to(largest * 2.0 ** -24, (8, LANES))


def pick(table, index):
    return jnp.take_along_axis(table, index, axis=1, mode="promise_in_bounds")


def turn_rows(vel_ref, out_ref, code_ref, packed_ref, mean_ref, table_ref, unit, got_packed, got_mean, base, count):
    for r in range(count):
        code = jnp.broadcast_to(code_ref[pl.ds(base + r, 1), :], (8, LANES))
        z = code & (DEPTH - 1)
        group = code >> 10
        for g in range(GROUPS):
            rows = slice(8 * g, 8 * g + 8)
            found = [pick(packed_ref[rows, :], z), pick(mean_ref[0, rows, :], z), pick(mean_ref[1, rows, :], z)]
            if g == 0:
                got = found
            else:
                here = group == g
                got = [jnp.where(here, new, old) for new, old in zip(found, got)]
        got_packed[8 * r:8 * r + 8, :] = got[0]
        got_mean[0, 8 * r:8 * r + 8, :] = got[1]
        got_mean[1, 8 * r:8 * r + 8, :] = got[2]
    for b in range(count // 8):
        rows = pl.ds(pl.multiple_of(base + 8 * b, 8), 8)
        code = code_ref[rows, :]
        sub = (code >> 7) & 7
        masks = [sub == k for k in range(8)]

        def choose(ref):
            value = ref[pl.ds(64 * b, 8, stride=8), :]
            for k in range(1, 8):
                value = jnp.where(masks[k], ref[pl.ds(64 * b + k, 8, stride=8), :], value)
            return value

        packed = choose(got_packed)
        index = packed & (NAXES - 1)
        mean = [(packed >> 6).astype(jnp.float32) * unit, choose(got_mean.at[0]), choose(got_mean.at[1])]
        axis = [pick(table_ref[c], index) for c in range(3)]
        vel = [vel_ref[c, rows, :] for c in range(3)]
        rel = [vel[c] - mean[c] for c in range(3)]
        along = (1.0 - turn_cos) * (axis[0] * rel[0] + axis[1] * rel[1] + axis[2] * rel[2])
        for c in range(3):
            d, e = (c + 1) % 3, (c + 2) % 3
            cross = axis[d] * rel[e] - axis[e] * rel[d]
            turned = mean[c] + turn_cos * rel[c] + turn_sin * cross + along * axis[c]
            out_ref[c, rows, :] = jnp.where(code < DEAD, turned, vel[c])


def turn_kernel(step, vel_ref, code_ref, axes_ref, table_ref, sums_ref, b_ref, a_ref, c_ref, d_ref, *rest):
    last = step == STEPS - 1
    if last:
        first = (rest[1], rest[0], rest[2], rest[3])
        out_ref, total_ref, index_ref, packed_ref, mean_ref, got_packed, got_mean = rest[4:]
    else:
        first = (a_ref, b_ref, c_ref, d_ref)
        out_ref, next_ref, na_ref, nb_ref, total_ref, index_ref, packed_ref, mean_ref, got_packed, got_mean, key_ref, pair_ref, acc_ref = rest
        fill_keys(code_ref[step + 1], key_ref, pair_ref)
        acc_ref[...] = jnp.zeros_like(acc_ref)
    unit = fill_fields(step, axes_ref, sums_ref, a_ref, b_ref, c_ref, d_ref, first, total_ref, index_ref, packed_ref, mean_ref)

    def turn_block(base):
        turn_rows(vel_ref, out_ref, code_ref.at[step], packed_ref, mean_ref, table_ref, unit, got_packed, got_mean, base, BLOCK)

    def body(turn, carry):
        base = pl.multiple_of(turn * BLOCK, BLOCK)
        if not last:
            scatter_rows(acc_ref, out_ref, key_ref, pair_ref, base - BLOCK, BLOCK)
        turn_block(base)
        return carry

    turn_block(0)
    lax.fori_loop(1, ROWS // BLOCK, body, 0)
    if not last:
        scatter_rows(acc_ref, out_ref, key_ref, pair_ref, ROWS - BLOCK, BLOCK)
        finish_sums(acc_ref, next_ref)
        write_faces(next_ref, na_ref, nb_ref)


HBM = pl.BlockSpec(memory_space=pltpu.HBM)
SMEM = pl.BlockSpec(memory_space=pltpu.SMEM)
VMEM = pl.BlockSpec(memory_space=pltpu.VMEM)


def f32(*shape):
    return jax.ShapeDtypeStruct(shape, jnp.float32)


def i32(*shape):
    return jax.ShapeDtypeStruct(shape, jnp.int32)


def scatter_scratch():
    return [
        pltpu.VMEM((ROWS, LANES), jnp.float32),
        pltpu.VMEM((ROWS, LANES), jnp.float32),
        pltpu.VMEM((WIDE, 2 * DEPTH), jnp.float32),
    ]


def scatter_call(live, offsets, vel, bins, axes, table):
    face = f32(FACE + AXROWS, LANES)
    out_shape = (f32(3, ROWS, LANES), i32(STEPS, ROWS, LANES), i32(*axes.shape), f32(3, 8, LANES), f32(SUMS, LANES), face, face)
    return pl.pallas_call(
        scatter_kernel,
        out_shape=out_shape,
        in_specs=[SMEM] + [HBM] * 5,
        out_specs=tuple([VMEM] * len(out_shape)),
        scratch_shapes=[pltpu.VMEM((STEPS, 3, ROWS, LANES), jnp.int32)] + scatter_scratch() + [
            pltpu.SMEM((STEPS, 3), jnp.int32),
            pltpu.SemaphoreType.DMA((6,)),
        ],
        compiler_params=pltpu.CompilerParams(vmem_limit_bytes=VMEM_LIMIT),
        name="scatter",
    )(live, offsets, vel, bins, axes, table)


def turn_call(step, *args):
    last = step == STEPS - 1
    out_shape = [f32(3, ROWS, LANES)]
    scratch = [
        pltpu.VMEM((SUMS, LANES), jnp.float32),
        pltpu.VMEM((8 * GROUPS, LANES), jnp.int32),
        pltpu.VMEM((8 * GROUPS, LANES), jnp.int32),
        pltpu.VMEM((2, 8 * GROUPS, LANES), jnp.float32),
        pltpu.VMEM((8 * BLOCK, LANES), jnp.int32),
        pltpu.VMEM((2, 8 * BLOCK, LANES), jnp.float32),
    ]
    if not last:
        out_shape += [f32(SUMS, LANES), f32(FACE, LANES), f32(FACE, LANES)]
        scratch += scatter_scratch()
    return pl.pallas_call(
        functools.partial(turn_kernel, step),
        out_shape=tuple(out_shape),
        in_specs=[VMEM] * len(args),
        out_specs=tuple([VMEM] * len(out_shape)),
        scratch_shapes=scratch,
        compiler_params=pltpu.CompilerParams(vmem_limit_bytes=VMEM_LIMIT),
        name="turn",
    )(*args)


def swaps(count_x, count_y):
    x_odd, x_even, y_odd, y_even = [], [], [], []
    for i in range(count_x):
        for j in range(count_y):
            here = i * count_y + j
            up = i + 1 if i % 2 == 1 else i - 1
            x_odd.append((here, up * count_y + j if 0 <= up < count_x else i * count_y + (j ^ 1)))
            x_even.append((here, (i ^ 1) * count_y + j))
            y_odd.append((here, i * count_y + ((j + 1 if j % 2 == 1 else j - 1) % count_y)))
            y_even.append((here, i * count_y + (j ^ 1)))
    return x_odd, x_even, y_odd, y_even


def y_messages(step, axes, sums, got_a, got_b):
    i = lax.axis_index("gx")
    odd_x = i % 2 == 1
    low_x = jnp.where(odd_x, got_b, got_a)
    high_x = jnp.where(odd_x, got_a, got_b)
    has_low, has_high = i > 0, i < lax.axis_size("gx") - 1
    ends = []
    for start in (0, 4 * CELLS_Y):
        rows = slice(start, start + 4)
        ends.append([
            sums[0:FACE][rows] + jnp.where(has_low, low_x[:FACE][rows], 0.0),
            sums[FACE:2 * FACE][rows] + jnp.where(has_high, high_x[:FACE][rows], 0.0),
            sums[2 * FACE:3 * FACE][rows],
        ])
    if step == 0:
        for s in range(STEPS):
            own = axes[s, :, 0].astype(jnp.float32)
            rows = [own[0:1], high_x[FACE + s * CELLS_Y:FACE + s * CELLS_Y + 1], own[1:2], own[1:2]]
            ends = [end + rows for end in ends]
    return [jnp.concatenate(end) for end in ends]


def per_device(perms, velocities, bins, offsets, axes, live):
    names = ("gx", "gy")
    x_odd, x_even, y_odd, y_even = perms
    odd_y = lax.axis_index("gy") % 2 == 1
    inputs = (offsets, velocities.reshape(3, ROWS, LANES), bins.reshape(3, STEPS, ROWS, LANES), axes, jnp.asarray(axis_table()))
    vel, code, axes, table, sums, a, b = scatter_call(live, *[pltpu.with_memory_space_constraint(x, pltpu.HBM) for x in inputs])
    first = ()
    for step in range(STEPS):
        got_b = lax.ppermute(b, names, x_even)
        got_a = lax.ppermute(a, names, x_odd)
        bottom, top = y_messages(step, axes, sums, got_a, got_b)
        got_d = lax.ppermute(jnp.where(odd_y, bottom, top), names, y_even)
        got_c = lax.ppermute(jnp.where(odd_y, top, bottom), names, y_odd)
        got = (got_b, got_a, got_c, got_d)
        done = turn_call(step, vel, code, axes, table, sums, *got, *first)
        if step < STEPS - 1:
            vel, sums, a, b = done
            first = got
        else:
            vel = done[0]
    return vel.reshape(velocities.shape)


def solution(mesh):
    placed = (
        P(None, "gx", "gy", None),
        P(None, None, "gx", "gy", None),
        P(),
        P(None, "gx", "gy", None),
        P("gx", "gy"),
    )
    perms = swaps(mesh.shape["gx"], mesh.shape["gy"])
    return jax.shard_map(
        functools.partial(per_device, perms), mesh=mesh, in_specs=placed, out_specs=P(None, "gx", "gy", None), check_vma=False
    )
```

```python
import functools
import math

import jax
import jax.numpy as jnp
import numpy as np
from jax import lax
from jax.experimental import pallas as pl
from jax.experimental.pallas import tpu as pltpu
from jax.sharding import PartitionSpec as P

NAXES = 64
STEPS = 2
SLOTS = 20480
LANES = 128
ROWS = SLOTS // LANES
DEPTH = 128
CELLS_X = 2
CELLS_Y = 16
PLANE = 16
EDGE = 3 * PLANE
GROUPS = 7
FACE = 4 * PLANE + 8
SUMS = 32 * GROUPS
EDGES = 24
WIDE = 8 * 28
AXROWS = STEPS * CELLS_Y
BLOCK = 80
LOWEST = 121
DEAD = 64 * DEPTH
VMEM_LIMIT = 40 * 1024 * 1024

turn_cos = math.cos(130.0 * math.pi / 180.0)
turn_sin = math.sin(130.0 * math.pi / 180.0)
golden = math.pi * (3.0 - math.sqrt(5.0))


def axis_table():
    index = np.arange(NAXES).astype(np.float32)
    height = (np.float32(1.0) - (np.float32(2.0) * index + np.float32(1.0)) / np.float32(NAXES)).astype(np.float32)
    radius = np.sqrt(np.float32(1.0) - height * height).astype(np.float32)
    angle = (index * np.float32(golden)).astype(np.float64)
    rows = np.stack([radius * np.cos(angle), radius * np.sin(angle), height]).astype(np.float32)
    padded = np.zeros((3, 1, LANES), np.float32)
    padded[:, 0, :NAXES] = rows
    return np.broadcast_to(padded, (3, 8, LANES)).copy()


def row_ids(shape):
    return lax.broadcasted_iota(jnp.int32, shape, 0)


def cell_code(bins_ref, step, offsets_ref, live, at_wall):
    shape = (ROWS, LANES)
    cell_x = (bins_ref[0] + offsets_ref[step, 0]) >> 2
    cell_x = jnp.where(at_wall, jnp.minimum(cell_x, CELLS_X - 1), cell_x)
    cell_y = (bins_ref[1] + offsets_ref[step, 1]) >> 2
    cell_z = ((bins_ref[2] + offsets_ref[step, 2]) >> 2) & (DEPTH - 1)
    plane = jnp.where(cell_x == 1, 0, 1 + (cell_x >> 1))
    particle = row_ids(shape) * LANES + lax.broadcasted_iota(jnp.int32, shape, 1)
    at_edge = (cell_y == 0) | (cell_y == CELLS_Y)
    column = jnp.where(at_edge, EDGE + 2 * plane + (cell_y >> 4), PLANE * plane + cell_y - 1)
    code = column * DEPTH + cell_z
    return jnp.where(particle < live, code, code + DEAD)


def fill_keys(code, key_ref, pair_ref):
    key_ref[...] = (code & 255).astype(jnp.float32)
    pair_ref[...] = (code >> 8).astype(jnp.float32)


def hot_row(key_ref, row):
    key = jnp.broadcast_to(key_ref[row, :], (16, LANES)).astype(jnp.bfloat16)
    one = jnp.ones((16, LANES), jnp.bfloat16)
    zero = jnp.zeros((16, LANES), jnp.bfloat16)
    ids = [(row_ids((16, LANES)) + 16 * t).astype(jnp.float32).astype(jnp.bfloat16) for t in range(16)]
    return jnp.concatenate([jnp.where(key == ids[t], one, zero) for t in range(16)], axis=0)


def spread_row(vel_ref, pair_ref, row):
    sub = row_ids((8, LANES))
    half = row_ids((16, LANES)) >> 3
    zero = jnp.zeros((16, LANES), jnp.bfloat16)
    part = [jnp.broadcast_to(vel_ref[c, row, :], (8, LANES)) for c in range(3)]
    full = jnp.where((sub == 0) | (sub == 3), part[0], jnp.where((sub == 1) | (sub == 4), part[1], part[2]))
    high = full.astype(jnp.bfloat16).astype(jnp.float32)
    data = jnp.where(sub < 3, high, jnp.where(sub < 6, full - high, jnp.where(sub == 6, 1.0, 0.0)))
    data = jnp.concatenate([data, data], axis=0).astype(jnp.bfloat16)
    pair = jnp.broadcast_to(pair_ref[row, :], (16, LANES)).astype(jnp.bfloat16)
    ids = [(half + 2 * t).astype(jnp.float32).astype(jnp.bfloat16) for t in range(WIDE // 16)]
    return jnp.concatenate([jnp.where(pair == ids[t], data, zero) for t in range(WIDE // 16)], axis=0)


def scatter_rows(acc_ref, vel_ref, key_ref, pair_ref, base, count):
    rows = [pl.ds(base + r, 1) for r in range(count)]
    spread = jnp.concatenate([spread_row(vel_ref, pair_ref, row) for row in rows], axis=1)
    hot = jnp.concatenate([hot_row(key_ref, row) for row in rows], axis=1)
    acc_ref[...] += lax.dot_general(spread, hot, (((1,), (1,)), ((), ())), preferred_element_type=jnp.float32)


def finish_sums(acc_ref, sums_ref):
    sub = row_ids((8, LANES))
    for q in range(SUMS // 8):
        halves = []
        for parity in range(2):
            part = acc_ref[8 * q:8 * q + 8, parity * DEPTH:(parity + 1) * DEPTH]
            moved = pltpu.roll(part, 5, 0)
            halves.append(jnp.where(sub < 3, part + moved, moved))
        sums_ref[8 * q:8 * q + 8, :] = jnp.where(sub < 4, halves[0], pltpu.roll(halves[1], 4, 0))


def write_faces(sums_ref, a_ref, b_ref):
    odd = lax.axis_index("gx") % 2 == 1
    for rows, low_at, high_at in ((4 * PLANE, 4 * PLANE, 8 * PLANE), (8, 4 * EDGE + 8, 4 * EDGE + 16)):
        start = 0 if rows > 8 else 4 * PLANE
        low = sums_ref[low_at:low_at + rows, :]
        high = sums_ref[high_at:high_at + rows, :]
        a_ref[start:start + rows, :] = jnp.where(odd, high, low)
        b_ref[start:start + rows, :] = jnp.where(odd, low, high)


def scatter_kernel(live_ref, offsets_hbm, vel_hbm, bins_hbm, axes_hbm, table_hbm,
                   vel_ref, code_ref, axes_ref, table_ref, sums_ref, a_ref, b_ref,
                   bins_ref, key_ref, pair_ref, acc_ref, offsets_ref, sems):
    copies = [
        pltpu.make_async_copy(offsets_hbm, offsets_ref, sems.at[0]),
        pltpu.make_async_copy(bins_hbm.at[:, 0], bins_ref.at[0], sems.at[1]),
        pltpu.make_async_copy(vel_hbm, vel_ref, sems.at[2]),
        pltpu.make_async_copy(bins_hbm.at[:, 1], bins_ref.at[1], sems.at[3]),
        pltpu.make_async_copy(axes_hbm, axes_ref, sems.at[4]),
        pltpu.make_async_copy(table_hbm, table_ref, sems.at[5]),
    ]
    for copy in copies:
        copy.start()
    acc_ref[...] = jnp.zeros_like(acc_ref)
    at_wall = lax.axis_index("gx") == lax.axis_size("gx") - 1
    for copy in copies[:2]:
        copy.wait()
    live = live_ref[0, 0]
    code = cell_code(bins_ref.at[0], 0, offsets_ref, live, at_wall)
    code_ref[0] = code
    fill_keys(code, key_ref, pair_ref)
    copies[2].wait()

    scatter_rows(acc_ref, vel_ref, key_ref, pair_ref, 0, ROWS)
    finish_sums(acc_ref, sums_ref)
    write_faces(sums_ref, a_ref, b_ref)
    for copy in copies[3:]:
        copy.wait()
    code_ref[1] = cell_code(bins_ref.at[1], 1, offsets_ref, live, at_wall)
    for step in range(STEPS):
        own = axes_ref[step, 0].astype(jnp.float32)
        a_ref[FACE + step * CELLS_Y:FACE + (step + 1) * CELLS_Y, :] = own
        b_ref[FACE + step * CELLS_Y:FACE + (step + 1) * CELLS_Y, :] = own


def pack_fields(total_ref, index_ref, first_ref, second_ref, start, groups):
    for g in range(groups):
        count = jnp.maximum(total_ref[pl.ds(start + 32 * g + 3, 8, stride=4), :], 1.0)
        mean = [total_ref[pl.ds(start + 32 * g + c, 8, stride=4), :] / count for c in range(3)]
        largest = jnp.maximum(jnp.maximum(jnp.abs(mean[0]), jnp.abs(mean[1])), jnp.abs(mean[2]))
        exponent = jnp.floor(jnp.log2(jnp.maximum(largest, 2.0 ** -120)) + 1.0001)
        scale = jnp.exp2(16.0 - exponent)
        x, y, z = [jnp.floor(m * scale + 0.5).astype(jnp.int32) for m in mean]
        z = z + 65536
        rows = slice(8 * g, 8 * g + 8)
        first_ref[rows, :] = (x << 15) | (index_ref[rows, :] << 9) | (z & 511)
        second_ref[rows, :] = (y << 15) | ((exponent.astype(jnp.int32) + LOWEST) << 8) | (z >> 9)


def unpack_fields(first, second):
    unit = jnp.exp2((((second >> 8) & 127) - (LOWEST + 16)).astype(jnp.float32))
    z = ((first & 511) | ((second & 255) << 9)) - 65536
    mean = [part.astype(jnp.float32) * unit for part in (first >> 15, second >> 15, z)]
    return mean, (first >> 9) & (NAXES - 1)


def pick(table, index):
    return jnp.take_along_axis(table, index, axis=1, mode="promise_in_bounds")


def gather_rows(code_ref, first_ref, second_ref, got_ref, base, count, start, groups):
    for r in range(count):
        code = jnp.broadcast_to(code_ref[pl.ds(base + r, 1), :], (8, LANES))
        z = code & (DEPTH - 1)
        group = code >> 10
        got = None
        for g in range(groups):
            rows = slice(8 * g, 8 * g + 8)
            found = [pick(first_ref[rows, :], z), pick(second_ref[rows, :], z)]
            got = found if got is None else [jnp.where(group == start + g, new, old) for new, old in zip(found, got)]
        got_ref[0, 8 * r:8 * r + 8, :] = got[0]
        got_ref[1, 8 * r:8 * r + 8, :] = got[1]


def choose_rows(code, got_ref, b):
    sub = (code >> 7) & 7
    masks = [sub == k for k in range(8)]
    words = []
    for w in range(2):
        value = got_ref[w, pl.ds(64 * b, 8, stride=8), :]
        for k in range(1, 8):
            value = jnp.where(masks[k], got_ref[w, pl.ds(64 * b + k, 8, stride=8), :], value)
        words.append(value)
    return words


def inner_kernel(step, code_ref, axes_ref, sums_ref, *rest):
    middle = len(rest) == 6
    if middle:
        start, groups = 0, 2
        out_ref, index_ref, first_ref, second_ref, got_ref, total_ref = rest
        index_ref[...] = jnp.zeros_like(index_ref)
        index_ref[0:CELLS_Y - 1, :] = axes_ref[step, 1, 1:CELLS_Y, :]
        total_ref[0:4 * PLANE, :] = sums_ref[0:4 * PLANE, :]
    else:
        start, groups = 2, 4
        b_ref, a_ref, first_b_ref, first_a_ref, before_ref, out_ref, index_ref, first_ref, second_ref, got_ref, total_ref = rest
        i = lax.axis_index("gx")
        odd = i % 2 == 1
        low = jnp.where(odd, b_ref[0:4 * PLANE, :], a_ref[0:4 * PLANE, :])
        high = jnp.where(odd, a_ref[0:4 * PLANE, :], b_ref[0:4 * PLANE, :])
        total_ref[0:4 * PLANE, :] = sums_ref[4 * PLANE:8 * PLANE, :] + jnp.where(i > 0, low, 0.0)
        total_ref[4 * PLANE:8 * PLANE, :] = sums_ref[8 * PLANE:12 * PLANE, :] + jnp.where(i < lax.axis_size("gx") - 1, high, 0.0)
        index_ref[...] = jnp.zeros_like(index_ref)
        index_ref[0:CELLS_Y - 1, :] = axes_ref[step, 0, 1:CELLS_Y, :]
        rows = slice(FACE + step * CELLS_Y + 1, FACE + (step + 1) * CELLS_Y)
        index_ref[PLANE:PLANE + CELLS_Y - 1, :] = jnp.where(odd, first_a_ref[rows, :], first_b_ref[rows, :]).astype(jnp.int32)
    pack_fields(total_ref, index_ref, first_ref, second_ref, 0, groups)

    def body(turn, carry):
        base = pl.multiple_of(turn * BLOCK, BLOCK)
        gather_rows(code_ref.at[step], first_ref, second_ref, got_ref, base, BLOCK, start, groups)
        for b in range(BLOCK // 8):
            rows = pl.ds(pl.multiple_of(base + 8 * b, 8), 8)
            code = code_ref[step, rows, :]
            for w, word in enumerate(choose_rows(code, got_ref, b)):
                out_ref[w, rows, :] = word if middle else jnp.where(code < start * 8 * DEPTH, before_ref[w, rows, :], word)
        return carry

    lax.fori_loop(0, ROWS // BLOCK, body, 0)


def turn_kernel(step, vel_ref, code_ref, axes_ref, table_ref, words_ref, edge_ref, c_ref, d_ref, first_edge_ref, first_c_ref, first_d_ref, *rest):
    last = step == STEPS - 1
    out_ref, total_ref, index_ref, first_ref, second_ref, got_ref = rest[:1] + rest[-8 + 3 * last:][:5]
    if not last:
        next_ref, na_ref, nb_ref = rest[1:4]
        key_ref, pair_ref, acc_ref = rest[-3:]
        fill_keys(code_ref[step + 1], key_ref, pair_ref)
        acc_ref[...] = jnp.zeros_like(acc_ref)
    odd = lax.axis_index("gy") % 2 == 1
    sub = row_ids((8, LANES))
    total_ref[...] = jnp.zeros_like(total_ref)
    index_ref[...] = jnp.zeros_like(index_ref)
    index_rows = slice(EDGES + 4 * step, EDGES + 4 * step + 4)
    index_low = first_edge_ref[index_rows, :].astype(jnp.int32)
    index_high = jnp.where(odd, first_c_ref[index_rows, :], first_d_ref[index_rows, :]).astype(jnp.int32)
    for plane in range(3):
        rows = slice(8 * plane, 8 * plane + 8)
        low = jnp.where(odd, d_ref[rows, :], c_ref[rows, :])
        high = jnp.where(odd, c_ref[rows, :], d_ref[rows, :])
        total_ref[rows, :] = edge_ref[rows, :] + pltpu.roll(jnp.where(sub < 4, high, low), 4, 0)
        index_ref[2 * plane:2 * plane + 1, :] = index_low[plane:plane + 1, :]
        index_ref[2 * plane + 1:2 * plane + 2, :] = index_high[plane:plane + 1, :]
    pack_fields(total_ref, index_ref, first_ref, second_ref, 0, 1)

    def body(turn, carry):
        base = pl.multiple_of(turn * BLOCK, BLOCK)
        gather_rows(code_ref.at[step], first_ref, second_ref, got_ref, base, BLOCK, GROUPS - 1, 1)
        for b in range(BLOCK // 8):
            rows = pl.ds(pl.multiple_of(base + 8 * b, 8), 8)
            code = code_ref[step, rows, :]
            words = [jnp.where(code < EDGE * DEPTH, words_ref[w, rows, :], word) for w, word in enumerate(choose_rows(code, got_ref, b))]
            mean, index = unpack_fields(*words)
            axis = [pick(table_ref[c], index) for c in range(3)]
            vel = [vel_ref[c, rows, :] for c in range(3)]
            rel = [vel[c] - mean[c] for c in range(3)]
            along = (1.0 - turn_cos) * (axis[0] * rel[0] + axis[1] * rel[1] + axis[2] * rel[2])
            for c in range(3):
                d, e = (c + 1) % 3, (c + 2) % 3
                cross = axis[d] * rel[e] - axis[e] * rel[d]
                turned = mean[c] + turn_cos * rel[c] + turn_sin * cross + along * axis[c]
                out_ref[c, rows, :] = jnp.where(code < DEAD, turned, vel[c])
        return carry

    lax.fori_loop(0, ROWS // BLOCK, body, 0)
    if not last:
        scatter_rows(acc_ref, out_ref, key_ref, pair_ref, 0, ROWS)
        finish_sums(acc_ref, next_ref)
        write_faces(next_ref, na_ref, nb_ref)


HBM = pl.BlockSpec(memory_space=pltpu.HBM)
SMEM = pl.BlockSpec(memory_space=pltpu.SMEM)
VMEM = pl.BlockSpec(memory_space=pltpu.VMEM)


def f32(*shape):
    return jax.ShapeDtypeStruct(shape, jnp.float32)


def i32(*shape):
    return jax.ShapeDtypeStruct(shape, jnp.int32)


def scatter_scratch():
    return [
        pltpu.VMEM((ROWS, LANES), jnp.float32),
        pltpu.VMEM((ROWS, LANES), jnp.float32),
        pltpu.VMEM((WIDE, 2 * DEPTH), jnp.float32),
    ]


def scatter_call(live, offsets, vel, bins, axes, table):
    face = f32(FACE + AXROWS, LANES)
    out_shape = (f32(3, ROWS, LANES), i32(STEPS, ROWS, LANES), i32(*axes.shape), f32(3, 8, LANES), f32(SUMS, LANES), face, face)
    return pl.pallas_call(
        scatter_kernel,
        out_shape=out_shape,
        in_specs=[SMEM] + [HBM] * 5,
        out_specs=tuple([VMEM] * len(out_shape)),
        scratch_shapes=[pltpu.VMEM((STEPS, 3, ROWS, LANES), jnp.int32)] + scatter_scratch() + [
            pltpu.SMEM((STEPS, 3), jnp.int32),
            pltpu.SemaphoreType.DMA((6,)),
        ],
        compiler_params=pltpu.CompilerParams(vmem_limit_bytes=VMEM_LIMIT),
        name="scatter",
    )(live, offsets, vel, bins, axes, table)


def field_scratch(groups):
    return [
        pltpu.VMEM((8 * groups, LANES), jnp.int32),
        pltpu.VMEM((8 * groups, LANES), jnp.int32),
        pltpu.VMEM((8 * groups, LANES), jnp.int32),
        pltpu.VMEM((2, 8 * BLOCK, LANES), jnp.int32),
    ]


def inner_call(step, *args):
    groups = 2 if len(args) == 3 else 4
    return pl.pallas_call(
        functools.partial(inner_kernel, step),
        out_shape=i32(2, ROWS, LANES),
        in_specs=[VMEM] * len(args),
        out_specs=VMEM,
        scratch_shapes=field_scratch(groups) + [pltpu.VMEM((32 * groups, LANES), jnp.float32)],
        compiler_params=pltpu.CompilerParams(vmem_limit_bytes=VMEM_LIMIT),
        cost_estimate=pl.CostEstimate(flops=0, bytes_accessed=8000000, transcendentals=0),
        name="inner",
    )(*args)


def turn_call(step, *args):
    last = step == STEPS - 1
    out_shape = [f32(3, ROWS, LANES)]
    scratch = [pltpu.VMEM((32, LANES), jnp.float32)] + field_scratch(1)
    if not last:
        out_shape += [f32(SUMS, LANES), f32(FACE, LANES), f32(FACE, LANES)]
        scratch += scatter_scratch()
    return pl.pallas_call(
        functools.partial(turn_kernel, step),
        out_shape=tuple(out_shape),
        in_specs=[VMEM] * len(args),
        out_specs=tuple([VMEM] * len(out_shape)),
        scratch_shapes=scratch,
        compiler_params=pltpu.CompilerParams(vmem_limit_bytes=VMEM_LIMIT),
        name="turn",
    )(*args)


def swaps(count_x, count_y):
    x_odd, x_even, y_odd, y_even = [], [], [], []
    for i in range(count_x):
        for j in range(count_y):
            here = i * count_y + j
            up = i + 1 if i % 2 == 1 else i - 1
            x_odd.append((here, up * count_y + j if 0 <= up < count_x else i * count_y + (j ^ 1)))
            x_even.append((here, (i ^ 1) * count_y + j))
            y_odd.append((here, i * count_y + ((j + 1 if j % 2 == 1 else j - 1) % count_y)))
            y_even.append((here, i * count_y + (j ^ 1)))
    return x_odd, x_even, y_odd, y_even


def edge_message(step, axes, sums, got_b, got_a):
    i = lax.axis_index("gx")
    odd = i % 2 == 1
    rows = slice(4 * PLANE, FACE)
    low = jnp.where(i > 0, jnp.where(odd, got_b[rows], got_a[rows]), 0.0)
    high = jnp.where(i < lax.axis_size("gx") - 1, jnp.where(odd, got_a[rows], got_b[rows]), 0.0)
    edge = sums[4 * EDGE:4 * EDGE + EDGES] + jnp.concatenate([jnp.zeros_like(low), low, high])
    if step > 0:
        return edge
    parts = [edge]
    for s in range(STEPS):
        own = axes[s, :, 0].astype(jnp.float32)
        row = FACE + s * CELLS_Y
        parts += [own[1:2], own[0:1], jnp.where(odd, got_a[row:row + 1], got_b[row:row + 1]), own[1:2]]
    return jnp.concatenate(parts)


def per_device(perms, velocities, bins, offsets, axes, live):
    names = ("gx", "gy")
    x_odd, x_even, y_odd, y_even = perms
    inputs = (offsets, velocities.reshape(3, ROWS, LANES), bins.reshape(3, STEPS, ROWS, LANES), axes, jnp.asarray(axis_table()))
    vel, code, axes, table, sums, a, b = scatter_call(live, *[pltpu.with_memory_space_constraint(x, pltpu.HBM) for x in inputs])
    for step in range(STEPS):
        got_b = lax.ppermute(b, names, x_even)
        got_a = lax.ppermute(a, names, x_odd)
        if step == 0:
            first_b, first_a = got_b, got_a
        words = inner_call(step, code, axes, sums)
        edge = edge_message(step, axes, sums, got_b, got_a)
        got_d = lax.ppermute(edge, names, y_even)
        got_c = lax.ppermute(edge, names, y_odd)
        if step == 0:
            first_edge, first_c, first_d = edge, got_c, got_d
        words = inner_call(step, code, axes, sums, got_b, got_a, first_b, first_a, words)
        done = turn_call(step, vel, code, axes, table, words, edge, got_c, got_d, first_edge, first_c, first_d)
        if step < STEPS - 1:
            vel, sums, a, b = done
        else:
            vel = done[0]
    return vel.reshape(velocities.shape)


def solution(mesh):
    placed = (
        P(None, "gx", "gy", None),
        P(None, None, "gx", "gy", None),
        P(),
        P(None, "gx", "gy", None),
        P("gx", "gy"),
    )
    perms = swaps(mesh.shape["gx"], mesh.shape["gy"])
    return jax.shard_map(
        functools.partial(per_device, perms), mesh=mesh, in_specs=placed, out_specs=P(None, "gx", "gy", None), check_vma=False
    )
```

```python
import functools
import math

import jax
import jax.numpy as jnp
import numpy as np
from jax import lax
from jax.experimental import pallas as pl
from jax.experimental.pallas import tpu as pltpu
from jax.sharding import PartitionSpec as P

NAXES = 64
STEPS = 2
SLOTS = 20480
LANES = 128
ROWS = SLOTS // LANES
DEPTH = 128
CELLS_X = 2
CELLS_Y = 16
PLANE = 16
EDGE = 3 * PLANE
GROUPS = 7
FACE = 4 * PLANE + 8
SUMS = 32 * GROUPS
EDGES = 24
WIDE = 8 * 28
AXROWS = STEPS * CELLS_Y
BLOCK = 80
LOWEST = 121
DEAD = 64 * DEPTH
VMEM_LIMIT = 40 * 1024 * 1024

turn_cos = math.cos(130.0 * math.pi / 180.0)
turn_sin = math.sin(130.0 * math.pi / 180.0)
golden = math.pi * (3.0 - math.sqrt(5.0))


def axis_table():
    index = np.arange(NAXES).astype(np.float32)
    height = (np.float32(1.0) - (np.float32(2.0) * index + np.float32(1.0)) / np.float32(NAXES)).astype(np.float32)
    radius = np.sqrt(np.float32(1.0) - height * height).astype(np.float32)
    angle = (index * np.float32(golden)).astype(np.float64)
    rows = np.stack([radius * np.cos(angle), radius * np.sin(angle), height]).astype(np.float32)
    padded = np.zeros((3, 1, LANES), np.float32)
    padded[:, 0, :NAXES] = rows
    return np.broadcast_to(padded, (3, 8, LANES)).copy()


def row_ids(shape):
    return lax.broadcasted_iota(jnp.int32, shape, 0)


def cell_code(bins_ref, step, offsets_ref, live, at_wall):
    shape = (ROWS, LANES)
    cell_x = (bins_ref[0] + offsets_ref[step, 0]) >> 2
    cell_x = jnp.where(at_wall, jnp.minimum(cell_x, CELLS_X - 1), cell_x)
    cell_y = (bins_ref[1] + offsets_ref[step, 1]) >> 2
    cell_z = ((bins_ref[2] + offsets_ref[step, 2]) >> 2) & (DEPTH - 1)
    plane = jnp.where(cell_x == 1, 0, 1 + (cell_x >> 1))
    particle = row_ids(shape) * LANES + lax.broadcasted_iota(jnp.int32, shape, 1)
    at_edge = (cell_y == 0) | (cell_y == CELLS_Y)
    column = jnp.where(at_edge, EDGE + 2 * plane + (cell_y >> 4), PLANE * plane + cell_y - 1)
    code = column * DEPTH + cell_z
    return jnp.where(particle < live, code, code + DEAD)


def fill_keys(code, key_ref, pair_ref):
    key_ref[...] = (code & 255).astype(jnp.float32)
    pair_ref[...] = (code >> 8).astype(jnp.float32)


def hot_row(key_ref, row):
    key = jnp.broadcast_to(key_ref[row, :], (16, LANES)).astype(jnp.bfloat16)
    one = jnp.ones((16, LANES), jnp.bfloat16)
    zero = jnp.zeros((16, LANES), jnp.bfloat16)
    ids = [(row_ids((16, LANES)) + 16 * t).astype(jnp.float32).astype(jnp.bfloat16) for t in range(16)]
    return jnp.concatenate([jnp.where(key == ids[t], one, zero) for t in range(16)], axis=0)


def spread_row(vel_ref, pair_ref, row):
    sub = row_ids((8, LANES))
    half = row_ids((16, LANES)) >> 3
    zero = jnp.zeros((16, LANES), jnp.bfloat16)
    part = [jnp.broadcast_to(vel_ref[c, row, :], (8, LANES)) for c in range(3)]
    full = jnp.where((sub == 0) | (sub == 3), part[0], jnp.where((sub == 1) | (sub == 4), part[1], part[2]))
    high = full.astype(jnp.bfloat16).astype(jnp.float32)
    data = jnp.where(sub < 3, high, jnp.where(sub < 6, full - high, jnp.where(sub == 6, 1.0, 0.0)))
    data = jnp.concatenate([data, data], axis=0).astype(jnp.bfloat16)
    pair = jnp.broadcast_to(pair_ref[row, :], (16, LANES)).astype(jnp.bfloat16)
    ids = [(half + 2 * t).astype(jnp.float32).astype(jnp.bfloat16) for t in range(WIDE // 16)]
    return jnp.concatenate([jnp.where(pair == ids[t], data, zero) for t in range(WIDE // 16)], axis=0)


def scatter_rows(acc_ref, vel_ref, key_ref, pair_ref):
    rows = [slice(r, r + 1) for r in range(ROWS)]
    spread = jnp.concatenate([spread_row(vel_ref, pair_ref, row) for row in rows], axis=1)
    hot = jnp.concatenate([hot_row(key_ref, row) for row in rows], axis=1)
    acc_ref[...] = lax.dot_general(hot, spread, (((1,), (1,)), ((), ())), preferred_element_type=jnp.float32).T


def finish_sums(acc_ref, sums_ref):
    sub = row_ids((8, LANES))
    for q in range(SUMS // 8):
        halves = []
        for parity in range(2):
            part = acc_ref[8 * q:8 * q + 8, parity * DEPTH:(parity + 1) * DEPTH]
            moved = pltpu.roll(part, 5, 0)
            halves.append(jnp.where(sub < 3, part + moved, moved))
        sums_ref[8 * q:8 * q + 8, :] = jnp.where(sub < 4, halves[0], pltpu.roll(halves[1], 4, 0))


def write_faces(sums_ref, a_ref, b_ref):
    odd = lax.axis_index("gx") % 2 == 1
    for rows, low_at, high_at in ((4 * PLANE, 4 * PLANE, 8 * PLANE), (8, 4 * EDGE + 8, 4 * EDGE + 16)):
        start = 0 if rows > 8 else 4 * PLANE
        low = sums_ref[low_at:low_at + rows, :]
        high = sums_ref[high_at:high_at + rows, :]
        a_ref[start:start + rows, :] = jnp.where(odd, high, low)
        b_ref[start:start + rows, :] = jnp.where(odd, low, high)


def scatter_kernel(live_ref, offsets_hbm, vel_hbm, bins_hbm, axes_hbm, table_hbm,
                   vel_ref, code_ref, axes_ref, table_ref, sums_ref, a_ref, b_ref,
                   bins_ref, key_ref, pair_ref, acc_ref, offsets_ref, sems):
    copies = [
        pltpu.make_async_copy(offsets_hbm, offsets_ref, sems.at[0]),
        pltpu.make_async_copy(bins_hbm.at[:, 0], bins_ref.at[0], sems.at[1]),
        pltpu.make_async_copy(vel_hbm, vel_ref, sems.at[2]),
        pltpu.make_async_copy(bins_hbm.at[:, 1], bins_ref.at[1], sems.at[3]),
        pltpu.make_async_copy(axes_hbm, axes_ref, sems.at[4]),
        pltpu.make_async_copy(table_hbm, table_ref, sems.at[5]),
    ]
    for copy in copies:
        copy.start()
    at_wall = lax.axis_index("gx") == lax.axis_size("gx") - 1
    for copy in copies[:2]:
        copy.wait()
    live = live_ref[0, 0]
    code = cell_code(bins_ref.at[0], 0, offsets_ref, live, at_wall)
    code_ref[0] = code
    fill_keys(code, key_ref, pair_ref)
    for copy in copies[2:]:
        copy.wait()
    code_ref[1] = cell_code(bins_ref.at[1], 1, offsets_ref, live, at_wall)
    for step in range(STEPS):
        own = axes_ref[step, 0].astype(jnp.float32)
        a_ref[FACE + step * CELLS_Y:FACE + (step + 1) * CELLS_Y, :] = own
        b_ref[FACE + step * CELLS_Y:FACE + (step + 1) * CELLS_Y, :] = own
    scatter_rows(acc_ref, vel_ref, key_ref, pair_ref)
    finish_sums(acc_ref, sums_ref)
    write_faces(sums_ref, a_ref, b_ref)


def pack_fields(total_ref, index_ref, first_ref, second_ref, start, groups):
    for g in range(groups):
        count = jnp.maximum(total_ref[pl.ds(start + 32 * g + 3, 8, stride=4), :], 1.0)
        mean = [total_ref[pl.ds(start + 32 * g + c, 8, stride=4), :] / count for c in range(3)]
        largest = jnp.maximum(jnp.maximum(jnp.abs(mean[0]), jnp.abs(mean[1])), jnp.abs(mean[2]))
        exponent = jnp.floor(jnp.log2(jnp.maximum(largest, 2.0 ** -120)) + 1.0001)
        scale = jnp.exp2(16.0 - exponent)
        x, y, z = [jnp.floor(m * scale + 0.5).astype(jnp.int32) for m in mean]
        z = z + 65536
        rows = slice(8 * g, 8 * g + 8)
        first_ref[rows, :] = (x << 15) | (index_ref[rows, :] << 9) | (z & 511)
        second_ref[rows, :] = (y << 15) | ((exponent.astype(jnp.int32) + LOWEST) << 8) | (z >> 9)


def unpack_fields(first, second):
    unit = jnp.exp2((((second >> 8) & 127) - (LOWEST + 16)).astype(jnp.float32))
    z = ((first & 511) | ((second & 255) << 9)) - 65536
    mean = [part.astype(jnp.float32) * unit for part in (first >> 15, second >> 15, z)]
    return mean, (first >> 9) & (NAXES - 1)


def pick(table, index):
    return jnp.take_along_axis(table, index, axis=1, mode="promise_in_bounds")


def gather_rows(code_ref, first_ref, second_ref, got_ref, base, count, start, groups):
    for r in range(count):
        code = jnp.broadcast_to(code_ref[pl.ds(base + r, 1), :], (8, LANES))
        z = code & (DEPTH - 1)
        group = code >> 10
        got = None
        for g in range(groups):
            rows = slice(8 * g, 8 * g + 8)
            found = [pick(first_ref[rows, :], z), pick(second_ref[rows, :], z)]
            got = found if got is None else [jnp.where(group == start + g, new, old) for new, old in zip(found, got)]
        got_ref[0, 8 * r:8 * r + 8, :] = got[0]
        got_ref[1, 8 * r:8 * r + 8, :] = got[1]


def choose_rows(code, got_ref, b):
    sub = (code >> 7) & 7
    masks = [sub == k for k in range(8)]
    words = []
    for w in range(2):
        value = got_ref[w, pl.ds(64 * b, 8, stride=8), :]
        for k in range(1, 8):
            value = jnp.where(masks[k], got_ref[w, pl.ds(64 * b + k, 8, stride=8), :], value)
        words.append(value)
    return words


def inner_kernel(step, code_ref, axes_ref, sums_ref, *rest):
    middle = len(rest) == 6
    if middle:
        start, groups = 0, 2
        out_ref, index_ref, first_ref, second_ref, got_ref, total_ref = rest
        index_ref[...] = jnp.zeros_like(index_ref)
        index_ref[0:CELLS_Y - 1, :] = axes_ref[step, 1, 1:CELLS_Y, :]
        total_ref[0:4 * PLANE, :] = sums_ref[0:4 * PLANE, :]
    else:
        start, groups = 2, 4
        b_ref, a_ref, first_b_ref, first_a_ref, before_ref, out_ref, index_ref, first_ref, second_ref, got_ref, total_ref = rest
        i = lax.axis_index("gx")
        odd = i % 2 == 1
        low = jnp.where(odd, b_ref[0:4 * PLANE, :], a_ref[0:4 * PLANE, :])
        high = jnp.where(odd, a_ref[0:4 * PLANE, :], b_ref[0:4 * PLANE, :])
        total_ref[0:4 * PLANE, :] = sums_ref[4 * PLANE:8 * PLANE, :] + jnp.where(i > 0, low, 0.0)
        total_ref[4 * PLANE:8 * PLANE, :] = sums_ref[8 * PLANE:12 * PLANE, :] + jnp.where(i < lax.axis_size("gx") - 1, high, 0.0)
        index_ref[...] = jnp.zeros_like(index_ref)
        index_ref[0:CELLS_Y - 1, :] = axes_ref[step, 0, 1:CELLS_Y, :]
        rows = slice(FACE + step * CELLS_Y + 1, FACE + (step + 1) * CELLS_Y)
        index_ref[PLANE:PLANE + CELLS_Y - 1, :] = jnp.where(odd, first_a_ref[rows, :], first_b_ref[rows, :]).astype(jnp.int32)
    pack_fields(total_ref, index_ref, first_ref, second_ref, 0, groups)

    def body(turn, carry):
        base = pl.multiple_of(turn * BLOCK, BLOCK)
        gather_rows(code_ref.at[step], first_ref, second_ref, got_ref, base, BLOCK, start, groups)
        for b in range(BLOCK // 8):
            rows = pl.ds(pl.multiple_of(base + 8 * b, 8), 8)
            code = code_ref[step, rows, :]
            for w, word in enumerate(choose_rows(code, got_ref, b)):
                out_ref[w, rows, :] = word if middle else jnp.where(code < start * 8 * DEPTH, before_ref[w, rows, :], word)
        return carry

    lax.fori_loop(0, ROWS // BLOCK, body, 0)


def turn_kernel(step, vel_ref, code_ref, axes_ref, table_ref, words_ref, edge_ref, c_ref, d_ref, first_edge_ref, first_c_ref, first_d_ref, *rest):
    last = step == STEPS - 1
    out_ref, total_ref, index_ref, first_ref, second_ref, got_ref = rest[:1] + rest[-8 + 3 * last:][:5]
    if not last:
        next_ref, na_ref, nb_ref = rest[1:4]
        key_ref, pair_ref, acc_ref = rest[-3:]
        fill_keys(code_ref[step + 1], key_ref, pair_ref)
    odd = lax.axis_index("gy") % 2 == 1
    sub = row_ids((8, LANES))
    total_ref[...] = jnp.zeros_like(total_ref)
    index_ref[...] = jnp.zeros_like(index_ref)
    index_rows = slice(EDGES + 4 * step, EDGES + 4 * step + 4)
    index_low = first_edge_ref[index_rows, :].astype(jnp.int32)
    index_high = jnp.where(odd, first_c_ref[index_rows, :], first_d_ref[index_rows, :]).astype(jnp.int32)
    for plane in range(3):
        rows = slice(8 * plane, 8 * plane + 8)
        low = jnp.where(odd, d_ref[rows, :], c_ref[rows, :])
        high = jnp.where(odd, c_ref[rows, :], d_ref[rows, :])
        total_ref[rows, :] = edge_ref[rows, :] + pltpu.roll(jnp.where(sub < 4, high, low), 4, 0)
        index_ref[2 * plane:2 * plane + 1, :] = index_low[plane:plane + 1, :]
        index_ref[2 * plane + 1:2 * plane + 2, :] = index_high[plane:plane + 1, :]
    pack_fields(total_ref, index_ref, first_ref, second_ref, 0, 1)

    def body(turn, carry):
        base = turn * BLOCK
        gather_rows(code_ref.at[step], first_ref, second_ref, got_ref, base, BLOCK, GROUPS - 1, 1)
        for b in range(BLOCK // 8):
            rows = pl.ds(base + 8 * b, 8)
            code = code_ref[step, rows, :]
            words = [jnp.where(code < EDGE * DEPTH, words_ref[w, rows, :], word) for w, word in enumerate(choose_rows(code, got_ref, b))]
            mean, index = unpack_fields(*words)
            axis = [pick(table_ref[c], index) for c in range(3)]
            vel = [vel_ref[c, rows, :] for c in range(3)]
            rel = [vel[c] - mean[c] for c in range(3)]
            along = (1.0 - turn_cos) * (axis[0] * rel[0] + axis[1] * rel[1] + axis[2] * rel[2])
            for c in range(3):
                d, e = (c + 1) % 3, (c + 2) % 3
                cross = axis[d] * rel[e] - axis[e] * rel[d]
                turned = mean[c] + turn_cos * rel[c] + turn_sin * cross + along * axis[c]
                out_ref[c, rows, :] = jnp.where(code < DEAD, turned, vel[c])
        return carry

    for turn in range(ROWS // BLOCK):
        body(turn, 0)
    if not last:
        scatter_rows(acc_ref, out_ref, key_ref, pair_ref)
        finish_sums(acc_ref, next_ref)
        write_faces(next_ref, na_ref, nb_ref)


HBM = pl.BlockSpec(memory_space=pltpu.HBM)
SMEM = pl.BlockSpec(memory_space=pltpu.SMEM)
VMEM = pl.BlockSpec(memory_space=pltpu.VMEM)


def f32(*shape):
    return jax.ShapeDtypeStruct(shape, jnp.float32)


def i32(*shape):
    return jax.ShapeDtypeStruct(shape, jnp.int32)


def scatter_scratch():
    return [
        pltpu.VMEM((ROWS, LANES), jnp.float32),
        pltpu.VMEM((ROWS, LANES), jnp.float32),
        pltpu.VMEM((WIDE, 2 * DEPTH), jnp.float32),
    ]


def scatter_call(live, offsets, vel, bins, axes, table):
    face = f32(FACE + AXROWS, LANES)
    out_shape = (f32(3, ROWS, LANES), i32(STEPS, ROWS, LANES), i32(*axes.shape), f32(3, 8, LANES), f32(SUMS, LANES), face, face)
    return pl.pallas_call(
        scatter_kernel,
        out_shape=out_shape,
        in_specs=[SMEM] + [HBM] * 5,
        out_specs=tuple([VMEM] * len(out_shape)),
        scratch_shapes=[pltpu.VMEM((STEPS, 3, ROWS, LANES), jnp.int32)] + scatter_scratch() + [
            pltpu.SMEM((STEPS, 3), jnp.int32),
            pltpu.SemaphoreType.DMA((6,)),
        ],
        compiler_params=pltpu.CompilerParams(vmem_limit_bytes=VMEM_LIMIT),
        name="scatter",
    )(live, offsets, vel, bins, axes, table)


def field_scratch(groups):
    return [
        pltpu.VMEM((8 * groups, LANES), jnp.int32),
        pltpu.VMEM((8 * groups, LANES), jnp.int32),
        pltpu.VMEM((8 * groups, LANES), jnp.int32),
        pltpu.VMEM((2, 8 * BLOCK, LANES), jnp.int32),
    ]


def inner_call(step, *args):
    groups = 2 if len(args) == 3 else 4
    return pl.pallas_call(
        functools.partial(inner_kernel, step),
        out_shape=i32(2, ROWS, LANES),
        in_specs=[VMEM] * len(args),
        out_specs=VMEM,
        scratch_shapes=field_scratch(groups) + [pltpu.VMEM((32 * groups, LANES), jnp.float32)],
        compiler_params=pltpu.CompilerParams(vmem_limit_bytes=VMEM_LIMIT),
        cost_estimate=pl.CostEstimate(flops=0, bytes_accessed=8000000, transcendentals=0),
        name="inner",
    )(*args)


def turn_call(step, *args):
    last = step == STEPS - 1
    out_shape = [f32(3, ROWS, LANES)]
    scratch = [pltpu.VMEM((32, LANES), jnp.float32)] + field_scratch(1)
    if not last:
        out_shape += [f32(SUMS, LANES), f32(FACE, LANES), f32(FACE, LANES)]
        scratch += scatter_scratch()
    return pl.pallas_call(
        functools.partial(turn_kernel, step),
        out_shape=tuple(out_shape),
        in_specs=[VMEM] * len(args),
        out_specs=tuple([VMEM] * len(out_shape)),
        scratch_shapes=scratch,
        compiler_params=pltpu.CompilerParams(vmem_limit_bytes=VMEM_LIMIT),
        name="turn",
    )(*args)


def swaps(count_x, count_y):
    x_odd, x_even, y_odd, y_even = [], [], [], []
    for i in range(count_x):
        for j in range(count_y):
            here = i * count_y + j
            up = i + 1 if i % 2 == 1 else i - 1
            x_odd.append((here, up * count_y + j if 0 <= up < count_x else i * count_y + (j ^ 1)))
            x_even.append((here, (i ^ 1) * count_y + j))
            y_odd.append((here, i * count_y + ((j + 1 if j % 2 == 1 else j - 1) % count_y)))
            y_even.append((here, i * count_y + (j ^ 1)))
    return x_odd, x_even, y_odd, y_even


def edge_message(step, axes, sums, got_b, got_a):
    i = lax.axis_index("gx")
    odd = i % 2 == 1
    rows = slice(4 * PLANE, FACE)
    low = jnp.where(i > 0, jnp.where(odd, got_b[rows], got_a[rows]), 0.0)
    high = jnp.where(i < lax.axis_size("gx") - 1, jnp.where(odd, got_a[rows], got_b[rows]), 0.0)
    edge = sums[4 * EDGE:4 * EDGE + EDGES] + jnp.concatenate([jnp.zeros_like(low), low, high])
    if step > 0:
        return edge
    parts = [edge]
    for s in range(STEPS):
        own = axes[s, :, 0].astype(jnp.float32)
        row = FACE + s * CELLS_Y
        parts += [own[1:2], own[0:1], jnp.where(odd, got_a[row:row + 1], got_b[row:row + 1]), own[1:2]]
    return jnp.concatenate(parts)


def per_device(perms, velocities, bins, offsets, axes, live):
    names = ("gx", "gy")
    x_odd, x_even, y_odd, y_even = perms
    inputs = (offsets, velocities.reshape(3, ROWS, LANES), bins.reshape(3, STEPS, ROWS, LANES), axes, jnp.asarray(axis_table()))
    vel, code, axes, table, sums, a, b = scatter_call(live, *[pltpu.with_memory_space_constraint(x, pltpu.HBM) for x in inputs])
    for step in range(STEPS):
        got_b = lax.ppermute(b, names, x_even)
        got_a = lax.ppermute(a, names, x_odd)
        if step == 0:
            first_b, first_a = got_b, got_a
        words = inner_call(step, code, axes, sums)
        got_b, got_a, words = lax.optimization_barrier((got_b, got_a, words))
        edge = edge_message(step, axes, sums, got_b, got_a)
        got_d = lax.ppermute(edge, names, y_even)
        got_c = lax.ppermute(edge, names, y_odd)
        if step == 0:
            first_edge, first_c, first_d = edge, got_c, got_d
        words = inner_call(step, code, axes, sums, got_b, got_a, first_b, first_a, words)
        done = turn_call(step, vel, code, axes, table, words, edge, got_c, got_d, first_edge, first_c, first_d)
        if step < STEPS - 1:
            vel, sums, a, b = done
        else:
            vel = done[0]
    return vel.reshape(velocities.shape)


def solution(mesh):
    placed = (
        P(None, "gx", "gy", None),
        P(None, None, "gx", "gy", None),
        P(),
        P(None, "gx", "gy", None),
        P("gx", "gy"),
    )
    perms = swaps(mesh.shape["gx"], mesh.shape["gy"])
    return jax.shard_map(
        functools.partial(per_device, perms), mesh=mesh, in_specs=placed, out_specs=P(None, "gx", "gy", None), check_vma=False
    )
```

```python
import functools
import math

import jax
import jax.numpy as jnp
import numpy as np
from jax import lax
from jax.experimental import pallas as pl
from jax.experimental.pallas import tpu as pltpu
from jax.sharding import PartitionSpec as P

NAXES = 64
STEPS = 2
SLOTS = 20480
LANES = 128
ROWS = SLOTS // LANES
DEPTH = 128
CELLS_X = 2
CELLS_Y = 16
PLANE = 16
EDGE = 3 * PLANE
GROUPS = 7
FACE = 4 * PLANE + 8
SUMS = 32 * GROUPS
EDGES = 24
WIDE = 8 * 28
AXROWS = STEPS * CELLS_Y
FIRST = 112
LOWEST = 121
DEAD = 64 * DEPTH
VMEM_LIMIT = 40 * 1024 * 1024

turn_cos = math.cos(130.0 * math.pi / 180.0)
turn_sin = math.sin(130.0 * math.pi / 180.0)
golden = math.pi * (3.0 - math.sqrt(5.0))


def axis_table():
    index = np.arange(NAXES).astype(np.float32)
    height = (np.float32(1.0) - (np.float32(2.0) * index + np.float32(1.0)) / np.float32(NAXES)).astype(np.float32)
    radius = np.sqrt(np.float32(1.0) - height * height).astype(np.float32)
    angle = (index * np.float32(golden)).astype(np.float64)
    rows = np.stack([radius * np.cos(angle), radius * np.sin(angle), height]).astype(np.float32)
    padded = np.zeros((3, 1, LANES), np.float32)
    padded[:, 0, :NAXES] = rows
    return np.broadcast_to(padded, (3, 8, LANES)).copy()


def row_ids(shape):
    return lax.broadcasted_iota(jnp.int32, shape, 0)


def cell_code(bins_ref, step, offsets_ref, live, at_wall):
    shape = (ROWS, LANES)
    cell_x = (bins_ref[0] + offsets_ref[step, 0]) >> 2
    cell_x = jnp.where(at_wall, jnp.minimum(cell_x, CELLS_X - 1), cell_x)
    cell_y = (bins_ref[1] + offsets_ref[step, 1]) >> 2
    cell_z = ((bins_ref[2] + offsets_ref[step, 2]) >> 2) & (DEPTH - 1)
    plane = jnp.where(cell_x == 1, 0, 1 + (cell_x >> 1))
    particle = row_ids(shape) * LANES + lax.broadcasted_iota(jnp.int32, shape, 1)
    at_edge = (cell_y == 0) | (cell_y == CELLS_Y)
    column = jnp.where(at_edge, EDGE + 2 * plane + (cell_y >> 4), PLANE * plane + cell_y - 1)
    code = column * DEPTH + cell_z
    return jnp.where(particle < live, code, code + DEAD)


def fill_keys(code, key_ref, pair_ref):
    key_ref[...] = (code & 255).astype(jnp.float32)
    pair_ref[...] = (code >> 8).astype(jnp.float32)


def hot_row(key_ref, row):
    key = jnp.broadcast_to(key_ref[row, :], (16, LANES)).astype(jnp.bfloat16)
    one = jnp.ones((16, LANES), jnp.bfloat16)
    zero = jnp.zeros((16, LANES), jnp.bfloat16)
    ids = [(row_ids((16, LANES)) + 16 * t).astype(jnp.float32).astype(jnp.bfloat16) for t in range(16)]
    return jnp.concatenate([jnp.where(key == ids[t], one, zero) for t in range(16)], axis=0)


def spread_row(vel_ref, pair_ref, row):
    sub = row_ids((8, LANES))
    half = row_ids((16, LANES)) >> 3
    zero = jnp.zeros((16, LANES), jnp.bfloat16)
    part = [jnp.broadcast_to(vel_ref[c, row, :], (8, LANES)) for c in range(3)]
    full = jnp.where((sub == 0) | (sub == 3), part[0], jnp.where((sub == 1) | (sub == 4), part[1], part[2]))
    high = full.astype(jnp.bfloat16).astype(jnp.float32)
    data = jnp.where(sub < 3, high, jnp.where(sub < 6, full - high, jnp.where(sub == 6, 1.0, 0.0)))
    data = jnp.concatenate([data, data], axis=0).astype(jnp.bfloat16)
    pair = jnp.broadcast_to(pair_ref[row, :], (16, LANES)).astype(jnp.bfloat16)
    ids = [(half + 2 * t).astype(jnp.float32).astype(jnp.bfloat16) for t in range(WIDE // 16)]
    return jnp.concatenate([jnp.where(pair == ids[t], data, zero) for t in range(WIDE // 16)], axis=0)


def scatter_rows(acc_ref, vel_ref, key_ref, pair_ref, count):
    rows = [slice(r, r + 1) for r in range(count)]
    spread = jnp.concatenate([spread_row(vel_ref, pair_ref, row) for row in rows], axis=1)
    hot = jnp.concatenate([hot_row(key_ref, row) for row in rows], axis=1)
    acc_ref[...] = lax.dot_general(hot, spread, (((1,), (1,)), ((), ())), preferred_element_type=jnp.float32).T


def each_part(live_ref, body, otherwise=None):
    more = live_ref[0, 0] > FIRST * LANES

    @pl.when(more)
    def _():
        body(ROWS)

    @pl.when(jnp.logical_not(more))
    def _():
        body(FIRST)
        if otherwise is not None:
            otherwise()


def finish_sums(acc_ref, sums_ref):
    sub = row_ids((8, LANES))
    for q in range(SUMS // 8):
        halves = []
        for parity in range(2):
            part = acc_ref[8 * q:8 * q + 8, parity * DEPTH:(parity + 1) * DEPTH]
            moved = pltpu.roll(part, 5, 0)
            halves.append(jnp.where(sub < 3, part + moved, moved))
        sums_ref[8 * q:8 * q + 8, :] = jnp.where(sub < 4, halves[0], pltpu.roll(halves[1], 4, 0))


def write_faces(sums_ref, a_ref, b_ref):
    odd = lax.axis_index("gx") % 2 == 1
    for rows, low_at, high_at in ((4 * PLANE, 4 * PLANE, 8 * PLANE), (8, 4 * EDGE + 8, 4 * EDGE + 16)):
        start = 0 if rows > 8 else 4 * PLANE
        low = sums_ref[low_at:low_at + rows, :]
        high = sums_ref[high_at:high_at + rows, :]
        a_ref[start:start + rows, :] = jnp.where(odd, high, low)
        b_ref[start:start + rows, :] = jnp.where(odd, low, high)


def scatter_kernel(live_ref, offsets_hbm, vel_hbm, bins_hbm, axes_hbm, table_hbm,
                   vel_ref, code_ref, axes_ref, table_ref, sums_ref, a_ref, b_ref,
                   bins_ref, key_ref, pair_ref, acc_ref, offsets_ref, sems):
    copies = [
        pltpu.make_async_copy(offsets_hbm, offsets_ref, sems.at[0]),
        pltpu.make_async_copy(bins_hbm.at[:, 0], bins_ref.at[0], sems.at[1]),
        pltpu.make_async_copy(vel_hbm, vel_ref, sems.at[2]),
        pltpu.make_async_copy(bins_hbm.at[:, 1], bins_ref.at[1], sems.at[3]),
        pltpu.make_async_copy(axes_hbm, axes_ref, sems.at[4]),
        pltpu.make_async_copy(table_hbm, table_ref, sems.at[5]),
    ]
    for copy in copies:
        copy.start()
    at_wall = lax.axis_index("gx") == lax.axis_size("gx") - 1
    for copy in copies[:2]:
        copy.wait()
    live = live_ref[0, 0]
    code = cell_code(bins_ref.at[0], 0, offsets_ref, live, at_wall)
    code_ref[0] = code
    fill_keys(code, key_ref, pair_ref)
    for copy in copies[2:]:
        copy.wait()
    code_ref[1] = cell_code(bins_ref.at[1], 1, offsets_ref, live, at_wall)
    for step in range(STEPS):
        own = axes_ref[step, 0].astype(jnp.float32)
        a_ref[FACE + step * CELLS_Y:FACE + (step + 1) * CELLS_Y, :] = own
        b_ref[FACE + step * CELLS_Y:FACE + (step + 1) * CELLS_Y, :] = own
    each_part(live_ref, functools.partial(scatter_rows, acc_ref, vel_ref, key_ref, pair_ref))
    finish_sums(acc_ref, sums_ref)
    write_faces(sums_ref, a_ref, b_ref)


def pack_fields(total_ref, index_ref, first_ref, second_ref, start, groups):
    for g in range(groups):
        count = jnp.maximum(total_ref[pl.ds(start + 32 * g + 3, 8, stride=4), :], 1.0)
        mean = [total_ref[pl.ds(start + 32 * g + c, 8, stride=4), :] / count for c in range(3)]
        largest = jnp.maximum(jnp.maximum(jnp.abs(mean[0]), jnp.abs(mean[1])), jnp.abs(mean[2]))
        exponent = jnp.floor(jnp.log2(jnp.maximum(largest, 2.0 ** -120)) + 1.0001)
        scale = jnp.exp2(16.0 - exponent)
        x, y, z = [jnp.floor(m * scale + 0.5).astype(jnp.int32) for m in mean]
        z = z + 65536
        rows = slice(8 * g, 8 * g + 8)
        first_ref[rows, :] = (x << 15) | (index_ref[rows, :] << 9) | (z & 511)
        second_ref[rows, :] = (y << 15) | ((exponent.astype(jnp.int32) + LOWEST) << 8) | (z >> 9)


def unpack_fields(first, second):
    unit = jnp.exp2((((second >> 8) & 127) - (LOWEST + 16)).astype(jnp.float32))
    z = ((first & 511) | ((second & 255) << 9)) - 65536
    mean = [part.astype(jnp.float32) * unit for part in (first >> 15, second >> 15, z)]
    return mean, (first >> 9) & (NAXES - 1)


def pick(table, index):
    return jnp.take_along_axis(table, index, axis=1, mode="promise_in_bounds")


def gather_rows(code_ref, first_ref, second_ref, got_ref, count, start, groups):
    for r in range(count):
        code = jnp.broadcast_to(code_ref[r:r + 1, :], (8, LANES))
        z = code & (DEPTH - 1)
        group = code >> 10
        got = None
        for g in range(groups):
            rows = slice(8 * g, 8 * g + 8)
            found = [pick(first_ref[rows, :], z), pick(second_ref[rows, :], z)]
            got = found if got is None else [jnp.where(group == start + g, new, old) for new, old in zip(found, got)]
        got_ref[0, 8 * r:8 * r + 8, :] = got[0]
        got_ref[1, 8 * r:8 * r + 8, :] = got[1]


def choose_rows(code, got_ref, b):
    sub = (code >> 7) & 7
    masks = [sub == k for k in range(8)]
    words = []
    for w in range(2):
        value = got_ref[w, pl.ds(64 * b, 8, stride=8), :]
        for k in range(1, 8):
            value = jnp.where(masks[k], got_ref[w, pl.ds(64 * b + k, 8, stride=8), :], value)
        words.append(value)
    return words


def inner_kernel(step, live_ref, code_ref, axes_ref, sums_ref, *rest):
    middle = len(rest) == 6
    if middle:
        start, groups = 0, 2
        out_ref, index_ref, first_ref, second_ref, got_ref, total_ref = rest
        index_ref[...] = jnp.zeros_like(index_ref)
        index_ref[0:CELLS_Y - 1, :] = axes_ref[step, 1, 1:CELLS_Y, :]
        total_ref[0:4 * PLANE, :] = sums_ref[0:4 * PLANE, :]
    else:
        start, groups = 2, 4
        b_ref, a_ref, first_b_ref, first_a_ref, before_ref, out_ref, index_ref, first_ref, second_ref, got_ref, total_ref = rest
        i = lax.axis_index("gx")
        odd = i % 2 == 1
        low = jnp.where(odd, b_ref[0:4 * PLANE, :], a_ref[0:4 * PLANE, :])
        high = jnp.where(odd, a_ref[0:4 * PLANE, :], b_ref[0:4 * PLANE, :])
        total_ref[0:4 * PLANE, :] = sums_ref[4 * PLANE:8 * PLANE, :] + jnp.where(i > 0, low, 0.0)
        total_ref[4 * PLANE:8 * PLANE, :] = sums_ref[8 * PLANE:12 * PLANE, :] + jnp.where(i < lax.axis_size("gx") - 1, high, 0.0)
        index_ref[...] = jnp.zeros_like(index_ref)
        index_ref[0:CELLS_Y - 1, :] = axes_ref[step, 0, 1:CELLS_Y, :]
        rows = slice(FACE + step * CELLS_Y + 1, FACE + (step + 1) * CELLS_Y)
        index_ref[PLANE:PLANE + CELLS_Y - 1, :] = jnp.where(odd, first_a_ref[rows, :], first_b_ref[rows, :]).astype(jnp.int32)
    pack_fields(total_ref, index_ref, first_ref, second_ref, 0, groups)

    def part(count):
        gather_rows(code_ref.at[step], first_ref, second_ref, got_ref, count, start, groups)
        for b in range(count // 8):
            rows = slice(8 * b, 8 * b + 8)
            code = code_ref[step, rows, :]
            for w, word in enumerate(choose_rows(code, got_ref, b)):
                out_ref[w, rows, :] = word if middle else jnp.where(code < start * 8 * DEPTH, before_ref[w, rows, :], word)

    each_part(live_ref, part)


def turn_kernel(step, live_ref, vel_ref, code_ref, axes_ref, table_ref, words_ref, edge_ref, c_ref, d_ref, first_edge_ref, first_c_ref, first_d_ref, *rest):
    last = step == STEPS - 1
    out_ref, total_ref, index_ref, first_ref, second_ref, got_ref = rest[:1] + rest[-8 + 3 * last:][:5]
    if not last:
        next_ref, na_ref, nb_ref = rest[1:4]
        key_ref, pair_ref, acc_ref = rest[-3:]
        fill_keys(code_ref[step + 1], key_ref, pair_ref)
    odd = lax.axis_index("gy") % 2 == 1
    sub = row_ids((8, LANES))
    total_ref[...] = jnp.zeros_like(total_ref)
    index_ref[...] = jnp.zeros_like(index_ref)
    index_rows = slice(EDGES + 4 * step, EDGES + 4 * step + 4)
    index_low = first_edge_ref[index_rows, :].astype(jnp.int32)
    index_high = jnp.where(odd, first_c_ref[index_rows, :], first_d_ref[index_rows, :]).astype(jnp.int32)
    for plane in range(3):
        rows = slice(8 * plane, 8 * plane + 8)
        low = jnp.where(odd, d_ref[rows, :], c_ref[rows, :])
        high = jnp.where(odd, c_ref[rows, :], d_ref[rows, :])
        total_ref[rows, :] = edge_ref[rows, :] + pltpu.roll(jnp.where(sub < 4, high, low), 4, 0)
        index_ref[2 * plane:2 * plane + 1, :] = index_low[plane:plane + 1, :]
        index_ref[2 * plane + 1:2 * plane + 2, :] = index_high[plane:plane + 1, :]
    pack_fields(total_ref, index_ref, first_ref, second_ref, 0, 1)

    def part(count):
        gather_rows(code_ref.at[step], first_ref, second_ref, got_ref, count, GROUPS - 1, 1)
        for b in range(count // 8):
            rows = slice(8 * b, 8 * b + 8)
            code = code_ref[step, rows, :]
            words = [jnp.where(code < EDGE * DEPTH, words_ref[w, rows, :], word) for w, word in enumerate(choose_rows(code, got_ref, b))]
            mean, index = unpack_fields(*words)
            axis = [pick(table_ref[c], index) for c in range(3)]
            vel = [vel_ref[c, rows, :] for c in range(3)]
            rel = [vel[c] - mean[c] for c in range(3)]
            along = (1.0 - turn_cos) * (axis[0] * rel[0] + axis[1] * rel[1] + axis[2] * rel[2])
            for c in range(3):
                d, e = (c + 1) % 3, (c + 2) % 3
                cross = axis[d] * rel[e] - axis[e] * rel[d]
                turned = mean[c] + turn_cos * rel[c] + turn_sin * cross + along * axis[c]
                out_ref[c, rows, :] = jnp.where(code < DEAD, turned, vel[c])
        if not last:
            scatter_rows(acc_ref, out_ref, key_ref, pair_ref, count)

    def keep():
        out_ref[:, FIRST:, :] = vel_ref[:, FIRST:, :]

    each_part(live_ref, part, keep)
    if not last:
        finish_sums(acc_ref, next_ref)
        write_faces(next_ref, na_ref, nb_ref)


HBM = pl.BlockSpec(memory_space=pltpu.HBM)
SMEM = pl.BlockSpec(memory_space=pltpu.SMEM)
VMEM = pl.BlockSpec(memory_space=pltpu.VMEM)


def f32(*shape):
    return jax.ShapeDtypeStruct(shape, jnp.float32)


def i32(*shape):
    return jax.ShapeDtypeStruct(shape, jnp.int32)


def scatter_scratch():
    return [
        pltpu.VMEM((ROWS, LANES), jnp.float32),
        pltpu.VMEM((ROWS, LANES), jnp.float32),
        pltpu.VMEM((WIDE, 2 * DEPTH), jnp.float32),
    ]


def scatter_call(live, offsets, vel, bins, axes, table):
    face = f32(FACE + AXROWS, LANES)
    out_shape = (f32(3, ROWS, LANES), i32(STEPS, ROWS, LANES), i32(*axes.shape), f32(3, 8, LANES), f32(SUMS, LANES), face, face)
    return pl.pallas_call(
        scatter_kernel,
        out_shape=out_shape,
        in_specs=[SMEM] + [HBM] * 5,
        out_specs=tuple([VMEM] * len(out_shape)),
        scratch_shapes=[pltpu.VMEM((STEPS, 3, ROWS, LANES), jnp.int32)] + scatter_scratch() + [
            pltpu.SMEM((STEPS, 3), jnp.int32),
            pltpu.SemaphoreType.DMA((6,)),
        ],
        compiler_params=pltpu.CompilerParams(vmem_limit_bytes=VMEM_LIMIT),
        name="scatter",
    )(live, offsets, vel, bins, axes, table)


def field_scratch(groups):
    return [
        pltpu.VMEM((8 * groups, LANES), jnp.int32),
        pltpu.VMEM((8 * groups, LANES), jnp.int32),
        pltpu.VMEM((8 * groups, LANES), jnp.int32),
        pltpu.VMEM((2, 8 * ROWS, LANES), jnp.int32),
    ]


def inner_call(step, *args):
    groups = 2 if len(args) == 4 else 4
    return pl.pallas_call(
        functools.partial(inner_kernel, step),
        out_shape=i32(2, ROWS, LANES),
        in_specs=[SMEM] + [VMEM] * (len(args) - 1),
        out_specs=VMEM,
        scratch_shapes=field_scratch(groups) + [pltpu.VMEM((32 * groups, LANES), jnp.float32)],
        compiler_params=pltpu.CompilerParams(vmem_limit_bytes=VMEM_LIMIT),
        cost_estimate=pl.CostEstimate(flops=0, bytes_accessed=8000000, transcendentals=0),
        name="inner",
    )(*args)


def turn_call(step, *args):
    last = step == STEPS - 1
    out_shape = [f32(3, ROWS, LANES)]
    scratch = [pltpu.VMEM((32, LANES), jnp.float32)] + field_scratch(1)
    if not last:
        out_shape += [f32(SUMS, LANES), f32(FACE, LANES), f32(FACE, LANES)]
        scratch += scatter_scratch()
    return pl.pallas_call(
        functools.partial(turn_kernel, step),
        out_shape=tuple(out_shape),
        in_specs=[SMEM] + [VMEM] * (len(args) - 1),
        out_specs=tuple([VMEM] * len(out_shape)),
        scratch_shapes=scratch,
        compiler_params=pltpu.CompilerParams(vmem_limit_bytes=VMEM_LIMIT),
        name="turn",
    )(*args)


def swaps(count_x, count_y):
    x_odd, x_even, y_odd, y_even = [], [], [], []
    for i in range(count_x):
        for j in range(count_y):
            here = i * count_y + j
            up = i + 1 if i % 2 == 1 else i - 1
            x_odd.append((here, up * count_y + j if 0 <= up < count_x else i * count_y + (j ^ 1)))
            x_even.append((here, (i ^ 1) * count_y + j))
            y_odd.append((here, i * count_y + ((j + 1 if j % 2 == 1 else j - 1) % count_y)))
            y_even.append((here, i * count_y + (j ^ 1)))
    return x_odd, x_even, y_odd, y_even


def edge_message(step, axes, sums, got_b, got_a):
    i = lax.axis_index("gx")
    odd = i % 2 == 1
    rows = slice(4 * PLANE, FACE)
    low = jnp.where(i > 0, jnp.where(odd, got_b[rows], got_a[rows]), 0.0)
    high = jnp.where(i < lax.axis_size("gx") - 1, jnp.where(odd, got_a[rows], got_b[rows]), 0.0)
    edge = sums[4 * EDGE:4 * EDGE + EDGES] + jnp.concatenate([jnp.zeros_like(low), low, high])
    if step > 0:
        return edge
    parts = [edge]
    for s in range(STEPS):
        own = axes[s, :, 0].astype(jnp.float32)
        row = FACE + s * CELLS_Y
        parts += [own[1:2], own[0:1], jnp.where(odd, got_a[row:row + 1], got_b[row:row + 1]), own[1:2]]
    return jnp.concatenate(parts)


def per_device(perms, velocities, bins, offsets, axes, live):
    names = ("gx", "gy")
    x_odd, x_even, y_odd, y_even = perms
    inputs = (offsets, velocities.reshape(3, ROWS, LANES), bins.reshape(3, STEPS, ROWS, LANES), axes, jnp.asarray(axis_table()))
    vel, code, axes, table, sums, a, b = scatter_call(live, *[pltpu.with_memory_space_constraint(x, pltpu.HBM) for x in inputs])
    for step in range(STEPS):
        got_b = lax.ppermute(b, names, x_even)
        got_a = lax.ppermute(a, names, x_odd)
        if step == 0:
            first_b, first_a = got_b, got_a
        words = inner_call(step, live, code, axes, sums)
        got_b, got_a, words = lax.optimization_barrier((got_b, got_a, words))
        edge = edge_message(step, axes, sums, got_b, got_a)
        got_d = lax.ppermute(edge, names, y_even)
        got_c = lax.ppermute(edge, names, y_odd)
        if step == 0:
            first_edge, first_c, first_d = edge, got_c, got_d
        words = inner_call(step, live, code, axes, sums, got_b, got_a, first_b, first_a, words)
        done = turn_call(step, live, vel, code, axes, table, words, edge, got_c, got_d, first_edge, first_c, first_d)
        if step < STEPS - 1:
            vel, sums, a, b = done
        else:
            vel = done[0]
    return vel.reshape(velocities.shape)


def solution(mesh):
    placed = (
        P(None, "gx", "gy", None),
        P(None, None, "gx", "gy", None),
        P(),
        P(None, "gx", "gy", None),
        P("gx", "gy"),
    )
    perms = swaps(mesh.shape["gx"], mesh.shape["gy"])
    return jax.shard_map(
        functools.partial(per_device, perms), mesh=mesh, in_specs=placed, out_specs=P(None, "gx", "gy", None), check_vma=False
    )
```

```python
import functools
import math

import jax
import jax.numpy as jnp
import numpy as np
from jax import lax
from jax.experimental import pallas as pl
from jax.experimental.pallas import tpu as pltpu
from jax.sharding import PartitionSpec as P

NAXES = 64
STEPS = 2
SLOTS = 20480
LANES = 128
ROWS = SLOTS // LANES
DEPTH = 128
CELLS_X = 2
CELLS_Y = 16
PLANE = 16
EDGE = 3 * PLANE
GROUPS = 7
FACE = 4 * PLANE + 8
SUMS = 32 * GROUPS
EDGES = 24
WIDE = 8 * 28
AXROWS = STEPS * CELLS_Y
FIRST = 112
LOWEST = 121
DEAD = 64 * DEPTH
VMEM_LIMIT = 40 * 1024 * 1024

turn_cos = math.cos(130.0 * math.pi / 180.0)
turn_sin = math.sin(130.0 * math.pi / 180.0)
golden = math.pi * (3.0 - math.sqrt(5.0))


def axis_table():
    index = np.arange(NAXES).astype(np.float32)
    height = (np.float32(1.0) - (np.float32(2.0) * index + np.float32(1.0)) / np.float32(NAXES)).astype(np.float32)
    radius = np.sqrt(np.float32(1.0) - height * height).astype(np.float32)
    angle = (index * np.float32(golden)).astype(np.float64)
    rows = np.stack([radius * np.cos(angle), radius * np.sin(angle), height]).astype(np.float32)
    padded = np.zeros((3, 1, LANES), np.float32)
    padded[:, 0, :NAXES] = rows
    return np.broadcast_to(padded, (3, 8, LANES)).copy()


def row_ids(shape):
    return lax.broadcasted_iota(jnp.int32, shape, 0)


def cell_code(bins_ref, step, offsets_ref, live, at_wall):
    shape = (ROWS, LANES)
    cell_x = (bins_ref[0] + offsets_ref[step, 0]) >> 2
    cell_x = jnp.where(at_wall, jnp.minimum(cell_x, CELLS_X - 1), cell_x)
    cell_y = (bins_ref[1] + offsets_ref[step, 1]) >> 2
    cell_z = ((bins_ref[2] + offsets_ref[step, 2]) >> 2) & (DEPTH - 1)
    plane = jnp.where(cell_x == 1, 0, 1 + (cell_x >> 1))
    particle = row_ids(shape) * LANES + lax.broadcasted_iota(jnp.int32, shape, 1)
    at_edge = (cell_y == 0) | (cell_y == CELLS_Y)
    column = jnp.where(at_edge, EDGE + 2 * plane + (cell_y >> 4), PLANE * plane + cell_y - 1)
    code = column * DEPTH + cell_z
    return jnp.where(particle < live, code, code + DEAD)


def fill_keys(code, key_ref, pair_ref):
    key_ref[...] = (code & 255).astype(jnp.float32)
    pair_ref[...] = (code >> 8).astype(jnp.float32)


def hot_row(key_ref, row):
    key = jnp.broadcast_to(key_ref[row, :], (16, LANES)).astype(jnp.bfloat16)
    one = jnp.ones((16, LANES), jnp.bfloat16)
    zero = jnp.zeros((16, LANES), jnp.bfloat16)
    ids = [(row_ids((16, LANES)) + 16 * t).astype(jnp.float32).astype(jnp.bfloat16) for t in range(16)]
    return jnp.concatenate([jnp.where(key == ids[t], one, zero) for t in range(16)], axis=0)


def spread_row(vel_ref, pair_ref, row):
    sub = row_ids((8, LANES))
    half = row_ids((16, LANES)) >> 3
    zero = jnp.zeros((16, LANES), jnp.bfloat16)
    part = [jnp.broadcast_to(vel_ref[c, row, :], (8, LANES)) for c in range(3)]
    full = jnp.where((sub == 0) | (sub == 3), part[0], jnp.where((sub == 1) | (sub == 4), part[1], part[2]))
    high = full.astype(jnp.bfloat16).astype(jnp.float32)
    data = jnp.where(sub < 3, high, jnp.where(sub < 6, full - high, jnp.where(sub == 6, 1.0, 0.0)))
    data = jnp.concatenate([data, data], axis=0).astype(jnp.bfloat16)
    pair = jnp.broadcast_to(pair_ref[row, :], (16, LANES)).astype(jnp.bfloat16)
    ids = [(half + 2 * t).astype(jnp.float32).astype(jnp.bfloat16) for t in range(WIDE // 16)]
    return jnp.concatenate([jnp.where(pair == ids[t], data, zero) for t in range(WIDE // 16)], axis=0)


def scatter_rows(acc_ref, vel_ref, key_ref, pair_ref, count):
    rows = [slice(r, r + 1) for r in range(count)]
    spread = jnp.concatenate([spread_row(vel_ref, pair_ref, row) for row in rows], axis=1)
    hot = jnp.concatenate([hot_row(key_ref, row) for row in rows], axis=1)
    acc_ref[...] = lax.dot_general(hot, spread, (((1,), (1,)), ((), ())), preferred_element_type=jnp.float32).T


def each_part(live_ref, body, otherwise=None):
    more = live_ref[0, 0] > FIRST * LANES

    @pl.when(more)
    def _():
        body(ROWS)

    @pl.when(jnp.logical_not(more))
    def _():
        body(FIRST)
        if otherwise is not None:
            otherwise()


def finish_sums(acc_ref, sums_ref):
    sub = row_ids((8, LANES))
    for q in range(SUMS // 8):
        halves = []
        for parity in range(2):
            part = acc_ref[8 * q:8 * q + 8, parity * DEPTH:(parity + 1) * DEPTH]
            moved = pltpu.roll(part, 5, 0)
            halves.append(jnp.where(sub < 3, part + moved, moved))
        sums_ref[8 * q:8 * q + 8, :] = jnp.where(sub < 4, halves[0], pltpu.roll(halves[1], 4, 0))


def write_faces(sums_ref, a_ref, b_ref):
    odd = lax.axis_index("gx") % 2 == 1
    for rows, low_at, high_at in ((4 * PLANE, 4 * PLANE, 8 * PLANE), (8, 4 * EDGE + 8, 4 * EDGE + 16)):
        start = 0 if rows > 8 else 4 * PLANE
        low = sums_ref[low_at:low_at + rows, :]
        high = sums_ref[high_at:high_at + rows, :]
        a_ref[start:start + rows, :] = jnp.where(odd, high, low)
        b_ref[start:start + rows, :] = jnp.where(odd, low, high)


def scatter_kernel(live_ref, offsets_hbm, vel_hbm, bins_hbm, axes_hbm, table_hbm,
                   vel_ref, code_ref, axes_ref, table_ref, sums_ref, a_ref, b_ref,
                   bins_ref, key_ref, pair_ref, acc_ref, offsets_ref, sems):
    copies = [
        pltpu.make_async_copy(offsets_hbm, offsets_ref, sems.at[0]),
        pltpu.make_async_copy(bins_hbm.at[:, 0], bins_ref.at[0], sems.at[1]),
        pltpu.make_async_copy(vel_hbm, vel_ref, sems.at[2]),
        pltpu.make_async_copy(bins_hbm.at[:, 1], bins_ref.at[1], sems.at[3]),
        pltpu.make_async_copy(axes_hbm, axes_ref, sems.at[4]),
        pltpu.make_async_copy(table_hbm, table_ref, sems.at[5]),
    ]
    for copy in copies:
        copy.start()
    at_wall = lax.axis_index("gx") == lax.axis_size("gx") - 1
    for copy in copies[:2]:
        copy.wait()
    live = live_ref[0, 0]
    code = cell_code(bins_ref.at[0], 0, offsets_ref, live, at_wall)
    code_ref[0] = code
    fill_keys(code, key_ref, pair_ref)
    for copy in copies[2:]:
        copy.wait()
    code_ref[1] = cell_code(bins_ref.at[1], 1, offsets_ref, live, at_wall)
    for step in range(STEPS):
        own = axes_ref[step, 0].astype(jnp.float32)
        a_ref[FACE + step * CELLS_Y:FACE + (step + 1) * CELLS_Y, :] = own
        b_ref[FACE + step * CELLS_Y:FACE + (step + 1) * CELLS_Y, :] = own
    each_part(live_ref, functools.partial(scatter_rows, acc_ref, vel_ref, key_ref, pair_ref))
    finish_sums(acc_ref, sums_ref)
    write_faces(sums_ref, a_ref, b_ref)


def pack_fields(total_ref, index_ref, first_ref, second_ref, start, groups):
    for g in range(groups):
        count = jnp.maximum(total_ref[pl.ds(start + 32 * g + 3, 8, stride=4), :], 1.0)
        mean = [total_ref[pl.ds(start + 32 * g + c, 8, stride=4), :] / count for c in range(3)]
        largest = jnp.maximum(jnp.maximum(jnp.abs(mean[0]), jnp.abs(mean[1])), jnp.abs(mean[2]))
        exponent = jnp.floor(jnp.log2(jnp.maximum(largest, 2.0 ** -120)) + 1.0001)
        scale = jnp.exp2(16.0 - exponent)
        x, y, z = [jnp.floor(m * scale + 0.5).astype(jnp.int32) for m in mean]
        z = z + 65536
        rows = slice(8 * g, 8 * g + 8)
        first_ref[rows, :] = (x << 15) | (index_ref[rows, :] << 9) | (z & 511)
        second_ref[rows, :] = (y << 15) | ((exponent.astype(jnp.int32) + LOWEST) << 8) | (z >> 9)


def unpack_fields(first, second):
    unit = jnp.exp2((((second >> 8) & 127) - (LOWEST + 16)).astype(jnp.float32))
    z = ((first & 511) | ((second & 255) << 9)) - 65536
    mean = [part.astype(jnp.float32) * unit for part in (first >> 15, second >> 15, z)]
    return mean, (first >> 9) & (NAXES - 1)


def pick(table, index):
    return jnp.take_along_axis(table, index, axis=1, mode="promise_in_bounds")


def gather_rows(code_ref, first_ref, second_ref, got_ref, count, start, groups):
    for r in range(count):
        code = jnp.broadcast_to(code_ref[r:r + 1, :], (8, LANES))
        z = code & (DEPTH - 1)
        group = code >> 10
        got = None
        for g in range(groups):
            rows = slice(8 * g, 8 * g + 8)
            found = [pick(first_ref[rows, :], z), pick(second_ref[rows, :], z)]
            got = found if got is None else [jnp.where(group == start + g, new, old) for new, old in zip(found, got)]
        got_ref[0, 8 * r:8 * r + 8, :] = got[0]
        got_ref[1, 8 * r:8 * r + 8, :] = got[1]


def choose_rows(code, got_ref, b):
    sub = (code >> 7) & 7
    masks = [sub == k for k in range(8)]
    words = []
    for w in range(2):
        value = got_ref[w, pl.ds(64 * b, 8, stride=8), :]
        for k in range(1, 8):
            value = jnp.where(masks[k], got_ref[w, pl.ds(64 * b + k, 8, stride=8), :], value)
        words.append(value)
    return words


def inner_kernel(step, live_ref, code_ref, axes_ref, sums_ref, *rest):
    middle = len(rest) == 6
    if middle:
        start, groups = 0, 2
        out_ref, index_ref, first_ref, second_ref, got_ref, total_ref = rest
        index_ref[...] = jnp.zeros_like(index_ref)
        index_ref[0:CELLS_Y - 1, :] = axes_ref[step, 1, 1:CELLS_Y, :]
        total_ref[0:4 * PLANE, :] = sums_ref[0:4 * PLANE, :]
    else:
        start, groups = 2, 4
        b_ref, a_ref, first_b_ref, first_a_ref, before_ref, out_ref, index_ref, first_ref, second_ref, got_ref, total_ref = rest
        i = lax.axis_index("gx")
        odd = i % 2 == 1
        low = jnp.where(odd, b_ref[0:4 * PLANE, :], a_ref[0:4 * PLANE, :])
        high = jnp.where(odd, a_ref[0:4 * PLANE, :], b_ref[0:4 * PLANE, :])
        total_ref[0:4 * PLANE, :] = sums_ref[4 * PLANE:8 * PLANE, :] + jnp.where(i > 0, low, 0.0)
        total_ref[4 * PLANE:8 * PLANE, :] = sums_ref[8 * PLANE:12 * PLANE, :] + jnp.where(i < lax.axis_size("gx") - 1, high, 0.0)
        index_ref[...] = jnp.zeros_like(index_ref)
        index_ref[0:CELLS_Y - 1, :] = axes_ref[step, 0, 1:CELLS_Y, :]
        rows = slice(FACE + step * CELLS_Y + 1, FACE + (step + 1) * CELLS_Y)
        index_ref[PLANE:PLANE + CELLS_Y - 1, :] = jnp.where(odd, first_a_ref[rows, :], first_b_ref[rows, :]).astype(jnp.int32)
    pack_fields(total_ref, index_ref, first_ref, second_ref, 0, groups)

    def part(count):
        gather_rows(code_ref.at[step], first_ref, second_ref, got_ref, count, start, groups)
        for b in range(count // 8):
            rows = slice(8 * b, 8 * b + 8)
            code = code_ref[step, rows, :]
            for w, word in enumerate(choose_rows(code, got_ref, b)):
                out_ref[w, rows, :] = word if middle else jnp.where(code < start * 8 * DEPTH, before_ref[w, rows, :], word)

    each_part(live_ref, part)


def turn_kernel(step, live_ref, vel_ref, code_ref, axes_ref, table_ref, words_ref, edge_ref, d_ref, c_ref, first_edge_ref, first_d_ref, first_c_ref, *rest):
    last = step == STEPS - 1
    out_ref, total_ref, index_ref, first_ref, second_ref, got_ref = rest[:1] + rest[-8 + 3 * last:][:5]
    if not last:
        next_ref, na_ref, nb_ref = rest[1:4]
        key_ref, pair_ref, acc_ref = rest[-3:]
        fill_keys(code_ref[step + 1], key_ref, pair_ref)
    odd = lax.axis_index("gy") % 2 == 1
    sub = row_ids((8, LANES))
    total_ref[...] = jnp.zeros_like(total_ref)
    index_ref[...] = jnp.zeros_like(index_ref)
    index_rows = slice(EDGES + 4 * step, EDGES + 4 * step + 4)
    index_low = first_edge_ref[index_rows, :].astype(jnp.int32)
    index_high = jnp.where(odd, first_c_ref[index_rows, :], first_d_ref[index_rows, :]).astype(jnp.int32)
    for plane in range(3):
        rows = slice(8 * plane, 8 * plane + 8)
        low = jnp.where(odd, d_ref[rows, :], c_ref[rows, :])
        high = jnp.where(odd, c_ref[rows, :], d_ref[rows, :])
        total_ref[rows, :] = edge_ref[rows, :] + pltpu.roll(jnp.where(sub < 4, high, low), 4, 0)
        index_ref[2 * plane:2 * plane + 1, :] = index_low[plane:plane + 1, :]
        index_ref[2 * plane + 1:2 * plane + 2, :] = index_high[plane:plane + 1, :]
    pack_fields(total_ref, index_ref, first_ref, second_ref, 0, 1)

    def part(count):
        gather_rows(code_ref.at[step], first_ref, second_ref, got_ref, count, GROUPS - 1, 1)
        for b in range(count // 8):
            rows = slice(8 * b, 8 * b + 8)
            code = code_ref[step, rows, :]
            words = [jnp.where(code < EDGE * DEPTH, words_ref[w, rows, :], word) for w, word in enumerate(choose_rows(code, got_ref, b))]
            mean, index = unpack_fields(*words)
            axis = [pick(table_ref[c], index) for c in range(3)]
            vel = [vel_ref[c, rows, :] for c in range(3)]
            rel = [vel[c] - mean[c] for c in range(3)]
            along = (1.0 - turn_cos) * (axis[0] * rel[0] + axis[1] * rel[1] + axis[2] * rel[2])
            for c in range(3):
                d, e = (c + 1) % 3, (c + 2) % 3
                cross = axis[d] * rel[e] - axis[e] * rel[d]
                turned = mean[c] + turn_cos * rel[c] + turn_sin * cross + along * axis[c]
                out_ref[c, rows, :] = jnp.where(code < DEAD, turned, vel[c])
        if not last:
            scatter_rows(acc_ref, out_ref, key_ref, pair_ref, count)

    def keep():
        out_ref[:, FIRST:, :] = vel_ref[:, FIRST:, :]

    each_part(live_ref, part, keep)
    if not last:
        finish_sums(acc_ref, next_ref)
        write_faces(next_ref, na_ref, nb_ref)


HBM = pl.BlockSpec(memory_space=pltpu.HBM)
SMEM = pl.BlockSpec(memory_space=pltpu.SMEM)
VMEM = pl.BlockSpec(memory_space=pltpu.VMEM)


def f32(*shape):
    return jax.ShapeDtypeStruct(shape, jnp.float32)


def i32(*shape):
    return jax.ShapeDtypeStruct(shape, jnp.int32)


def scatter_scratch():
    return [
        pltpu.VMEM((ROWS, LANES), jnp.float32),
        pltpu.VMEM((ROWS, LANES), jnp.float32),
        pltpu.VMEM((WIDE, 2 * DEPTH), jnp.float32),
    ]


def scatter_call(live, offsets, vel, bins, axes, table):
    face = f32(FACE + AXROWS, LANES)
    out_shape = (f32(3, ROWS, LANES), i32(STEPS, ROWS, LANES), i32(*axes.shape), f32(3, 8, LANES), f32(SUMS, LANES), face, face)
    return pl.pallas_call(
        scatter_kernel,
        out_shape=out_shape,
        in_specs=[SMEM] + [HBM] * 5,
        out_specs=tuple([VMEM] * len(out_shape)),
        scratch_shapes=[pltpu.VMEM((STEPS, 3, ROWS, LANES), jnp.int32)] + scatter_scratch() + [
            pltpu.SMEM((STEPS, 3), jnp.int32),
            pltpu.SemaphoreType.DMA((6,)),
        ],
        compiler_params=pltpu.CompilerParams(vmem_limit_bytes=VMEM_LIMIT),
        name="scatter",
    )(live, offsets, vel, bins, axes, table)


def field_scratch(groups):
    return [
        pltpu.VMEM((8 * groups, LANES), jnp.int32),
        pltpu.VMEM((8 * groups, LANES), jnp.int32),
        pltpu.VMEM((8 * groups, LANES), jnp.int32),
        pltpu.VMEM((2, 8 * ROWS, LANES), jnp.int32),
    ]


def inner_call(step, *args):
    groups = 2 if len(args) == 4 else 4
    return pl.pallas_call(
        functools.partial(inner_kernel, step),
        out_shape=i32(2, ROWS, LANES),
        in_specs=[SMEM] + [VMEM] * (len(args) - 1),
        out_specs=VMEM,
        scratch_shapes=field_scratch(groups) + [pltpu.VMEM((32 * groups, LANES), jnp.float32)],
        compiler_params=pltpu.CompilerParams(vmem_limit_bytes=VMEM_LIMIT),
        cost_estimate=pl.CostEstimate(flops=0, bytes_accessed=8000000, transcendentals=0),
        name="inner",
    )(*args)


def turn_call(step, *args):
    last = step == STEPS - 1
    out_shape = [f32(3, ROWS, LANES)]
    scratch = [pltpu.VMEM((32, LANES), jnp.float32)] + field_scratch(1)
    if not last:
        out_shape += [f32(SUMS, LANES), f32(FACE, LANES), f32(FACE, LANES)]
        scratch += scatter_scratch()
    return pl.pallas_call(
        functools.partial(turn_kernel, step),
        out_shape=tuple(out_shape),
        in_specs=[SMEM] + [VMEM] * (len(args) - 1),
        out_specs=tuple([VMEM] * len(out_shape)),
        scratch_shapes=scratch,
        compiler_params=pltpu.CompilerParams(vmem_limit_bytes=VMEM_LIMIT),
        name="turn",
    )(*args)


def swaps(count_x, count_y):
    x_odd, x_even, y_odd, y_even = [], [], [], []
    for i in range(count_x):
        for j in range(count_y):
            here = i * count_y + j
            up = i + 1 if i % 2 == 1 else i - 1
            x_odd.append((here, up * count_y + j if 0 <= up < count_x else i * count_y + (j ^ 1)))
            x_even.append((here, (i ^ 1) * count_y + j))
            y_odd.append((here, i * count_y + ((j + 1 if j % 2 == 1 else j - 1) % count_y)))
            y_even.append((here, i * count_y + (j ^ 1)))
    return x_odd, x_even, y_odd, y_even


def edge_message(step, axes, sums, got_b, got_a):
    i = lax.axis_index("gx")
    odd = i % 2 == 1
    rows = slice(4 * PLANE, FACE)
    low = jnp.where(i > 0, jnp.where(odd, got_b[rows], got_a[rows]), 0.0)
    high = jnp.where(i < lax.axis_size("gx") - 1, jnp.where(odd, got_a[rows], got_b[rows]), 0.0)
    edge = sums[4 * EDGE:4 * EDGE + EDGES] + jnp.concatenate([jnp.zeros_like(low), low, high])
    if step > 0:
        return edge
    parts = [edge]
    for s in range(STEPS):
        own = axes[s, :, 0].astype(jnp.float32)
        row = FACE + s * CELLS_Y
        parts += [own[1:2], own[0:1], jnp.where(odd, got_a[row:row + 1], got_b[row:row + 1]), own[1:2]]
    return jnp.concatenate(parts)


def per_device(perms, velocities, bins, offsets, axes, live):
    names = ("gx", "gy")
    x_odd, x_even, y_odd, y_even = perms
    inputs = (offsets, velocities.reshape(3, ROWS, LANES), bins.reshape(3, STEPS, ROWS, LANES), axes, jnp.asarray(axis_table()))
    vel, code, axes, table, sums, a, b = scatter_call(live, *[pltpu.with_memory_space_constraint(x, pltpu.HBM) for x in inputs])
    for step in range(STEPS):
        got_b = lax.ppermute(b, names, x_even)
        got_a = lax.ppermute(a, names, x_odd)
        if step == 0:
            first_b, first_a = got_b, got_a
        words = inner_call(step, live, code, axes, sums)
        got_b, got_a, words = lax.optimization_barrier((got_b, got_a, words))
        edge = edge_message(step, axes, sums, got_b, got_a)
        got_d = lax.ppermute(edge, names, y_even)
        got_c = lax.ppermute(edge, names, y_odd)
        if step == 0:
            first_edge, first_c, first_d = edge, got_c, got_d
        words = inner_call(step, live, code, axes, sums, got_b, got_a, first_b, first_a, words)
        done = turn_call(step, live, vel, code, axes, table, words, edge, got_d, got_c, first_edge, first_d, first_c)
        if step < STEPS - 1:
            vel, sums, a, b = done
        else:
            vel = done[0]
    return vel.reshape(velocities.shape)


def solution(mesh):
    placed = (
        P(None, "gx", "gy", None),
        P(None, None, "gx", "gy", None),
        P(),
        P(None, "gx", "gy", None),
        P("gx", "gy"),
    )
    perms = swaps(mesh.shape["gx"], mesh.shape["gy"])
    return jax.shard_map(
        functools.partial(per_device, perms), mesh=mesh, in_specs=placed, out_specs=P(None, "gx", "gy", None), check_vma=False
    )
```
